32 devices in a mesh: fsdp: 4 (over z), ctx: 4 (over y, x), tp: 2 (over core).
Axes of the slice: x: 2, y: 2, z: 4, core: 2. Of those that a mesh axis runs over, the one named last changes fastest.
Arguments:
- tokens: bfloat16 [8192, 2048], P(('fsdp', 'ctx')), may hold values from -6 to 6
- cotangent: bfloat16 [8192, 2048], P(('fsdp', 'ctx')), may hold values from -6 to 6
- lengths: int32 [4], P('fsdp'), may hold values from 1024 to 2048, as said below
- deal: int32 [4, 16], P('fsdp'), may hold values from 0 to 15, as said below
- attn_gain: bfloat16 [2048], P(('fsdp', 'ctx')), may hold values from 0.25 to 1.75
- w_query: bfloat16 [2048, 2048], P(('fsdp', 'ctx'), 'tp'), may hold values from -0.125 to 0.125
- w_key: bfloat16 [2048, 1024], P(('fsdp', 'ctx'), 'tp'), may hold values from -0.125 to 0.125
- w_value: bfloat16 [2048, 1024], P(('fsdp', 'ctx'), 'tp'), may hold values from -0.125 to 0.125
- w_out: bfloat16 [2048, 2048], P('tp', ('fsdp', 'ctx')), may hold values from -2 to 2
- query_gain: bfloat16 [128], replicated, may hold values from 0.25 to 1.75
- key_gain: bfloat16 [128], replicated, may hold values from 0.25 to 1.75
- ffn_gain: bfloat16 [2048], P(('fsdp', 'ctx')), may hold values from 0.25 to 1.75
- w_gate: bfloat16 [2048, 6144], P(('fsdp', 'ctx'), 'tp'), may hold values from -0.125 to 0.125
- w_up: bfloat16 [2048, 6144], P(('fsdp', 'ctx'), 'tp'), may hold values from -0.125 to 0.125
- w_down: bfloat16 [6144, 2048], P('tp', ('fsdp', 'ctx')), may hold values from -0.078125 to 0.078125
Outputs:
- output: bfloat16 [8192, 2048], P(('fsdp', 'ctx'))
- grad_tokens: float32 [8192, 2048], P(('fsdp', 'ctx'))
- grad_attn_gain: float32 [2048], P(('fsdp', 'ctx'))
- grad_w_query: float32 [2048, 2048], P(('fsdp', 'ctx'), 'tp')
- grad_w_key: float32 [2048, 1024], P(('fsdp', 'ctx'), 'tp')
- grad_w_value: float32 [2048, 1024], P(('fsdp', 'ctx'), 'tp')
- grad_w_out: float32 [2048, 2048], P('tp', ('fsdp', 'ctx'))
- grad_query_gain: float32 [128], replicated
- grad_key_gain: float32 [128], replicated
- grad_ffn_gain: float32 [2048], P(('fsdp', 'ctx'))
- grad_w_gate: float32 [2048, 6144], P(('fsdp', 'ctx'), 'tp')
- grad_w_up: float32 [2048, 6144], P(('fsdp', 'ctx'), 'tp')
- grad_w_down: float32 [6144, 2048], P('tp', ('fsdp', 'ctx'))
The draws below stay inside these ranges and needn't reach their ends.
Inputs may be any that keep to these rules, and one draw needn't show every extreme that they name: `lengths`: length of each sequence, counted in slots; in every draw one sequence has 2048 and another half of 2048. `deal`: each row is a permutation of the 16 blocks; the first slot block of each index of ctx (every 4-th, from 0) holds one of the blocks 0 to 3.
All inputs are finite; a program needn't handle non-finite values.
Results may differ from the reference program's by a relative error of at most 0.017.
Values may be sent and summed in bfloat16 or wider, within the bound.
No kernel may reach another device: no remote copies, remote signals or barrier semaphores. Data moves between devices by JAX's collectives and lax.ppermute only.
A program may use at most 256 MiB of HBM per device.

```python
import jax
import jax.numpy as jnp
from jax import lax

D = 2048
QH = 16
KVH = 8
HD = 128
FF = 6144
BLK = 128
BLK_DEV = 4
GROUPS = 4
BLOCKS = 16
SLOTS = 2048
TOKENS = 8192


def draw_lengths(key, part):
    key = jax.random.fold_in(key, 5)
    pick_key, size_key = jax.random.split(key)
    order = jax.random.permutation(pick_key, GROUPS)
    drawn = jax.random.randint(size_key, (GROUPS,), SLOTS // 2, SLOTS + 1)
    drawn = jnp.where(order == 0, SLOTS, drawn)
    drawn = jnp.where(order == 1, SLOTS // 2, drawn)
    return drawn.astype(jnp.int32)


def deal_row(row_key):
    ctx_count = BLOCKS // BLK_DEV
    first_key, rest_key = jax.random.split(row_key)
    leading = jax.random.permutation(first_key, ctx_count)
    trailing = ctx_count + jax.random.permutation(rest_key, BLOCKS - ctx_count)
    table = jnp.concatenate([leading[:, None], trailing.reshape(ctx_count, BLK_DEV - 1)], axis=1)
    return table.reshape(BLOCKS)


def draw_deal(key, part):
    key = jax.random.fold_in(key, 9)
    return jax.vmap(deal_row)(jax.random.split(key, GROUPS)).astype(jnp.int32)


def block_scale(own_key, extent, cuts, least, largest):
    loudness = 1.0
    for position, shards_of in cuts:
        heights = jax.random.uniform(jax.random.fold_in(jax.random.fold_in(own_key, 6), position), (shards_of,), jnp.float32, least / len(cuts), largest / len(cuts))
        loudness = loudness * jnp.repeat(jnp.exp(heights), extent[position] // shards_of).reshape((-1,) + (1,) * (len(extent) - 1 - position))
    return loudness


def centred(own_key, dims, spread, bound, pieces=(), held_as=jnp.bfloat16):
    level = block_scale(own_key, dims, pieces, -0.22, 0.18) if pieces else 1.0
    entries = jax.random.normal(own_key, dims, jnp.float32) * spread * level
    return jnp.minimum(jnp.maximum(entries, -bound), bound).astype(held_as)


def setup_inputs(seed: int = 0) -> dict:
    keys = jax.random.split(jax.random.key(seed), 16)
    return {
        "tokens": centred(keys[0], (TOKENS, D), 1.0, 6.0, ((0, 16),)),
        "cotangent": centred(keys[1], (TOKENS, D), 1.0, 6.0, ((0, 16),)),
        "lengths": draw_lengths(jax.random.fold_in(keys[15], 71), 0),
        "deal": draw_deal(jax.random.fold_in(keys[15], 71), 0),
        "attn_gain": jnp.clip(1.0 + 0.15 * jax.random.normal(keys[4], (D,), jnp.float32), 0.25, 1.75).astype(jnp.bfloat16),
        "w_query": centred(keys[5], (D, QH * HD), D ** -0.5, 0.125, ((0, 16), (1, 2))),
        "w_key": centred(keys[6], (D, KVH * HD), D ** -0.5, 0.125, ((0, 16), (1, 2))),
        "w_value": centred(keys[7], (D, KVH * HD), D ** -0.5, 0.125, ((0, 16), (1, 2))),
        "w_out": centred(keys[8], (QH * HD, D), (max(1, QH * HD * 8 // SLOTS)) ** -0.5, 2.0, ((0, 2), (1, 16))),
        "query_gain": jnp.clip(1.0 + 0.15 * jax.random.normal(keys[9], (HD,), jnp.float32), 0.25, 1.75).astype(jnp.bfloat16),
        "key_gain": jnp.clip(1.0 + 0.15 * jax.random.normal(keys[10], (HD,), jnp.float32), 0.25, 1.75).astype(jnp.bfloat16),
        "ffn_gain": jnp.clip(1.0 + 0.15 * jax.random.normal(keys[11], (D,), jnp.float32), 0.25, 1.75).astype(jnp.bfloat16),
        "w_gate": centred(keys[12], (D, FF), D ** -0.5, 0.125, ((0, 16), (1, 2))),
        "w_up": centred(keys[13], (D, FF), D ** -0.5, 0.125, ((0, 16), (1, 2))),
        "w_down": centred(keys[14], (FF, D), FF ** -0.5, 0.078125, ((0, 2), (1, 16))),
    }


EPS = 1e-06
THETA = 1000000.0
HIGHEST = lax.Precision.HIGHEST

@jax.custom_vjp
def low(v):
    return lax.optimization_barrier(v.astype(jnp.bfloat16)).astype(jnp.float32)

@jax.custom_vjp
def low_back(v):
    return v

def low_keep(v):
    return (low(v), None)

def low_pass(kept, grad):
    return (grad,)

def back_keep(v):
    return (v, None)

def back_low(kept, grad):
    return (low(grad),)
low.defvjp(low_keep, low_pass)
low_back.defvjp(back_keep, back_low)

def matmul(left, right):
    return jnp.dot(left, right, precision=HIGHEST)

def rms_norm(values, gain):
    return values * lax.rsqrt(lax.optimization_barrier(jnp.mean(values * values, axis=-1, keepdims=True)) + EPS) * gain

def rotary_tables(positions, head_size):
    frequency = THETA ** (-(jnp.arange(head_size // 2, dtype=jnp.float32) * 2.0 / head_size))
    angles = positions.astype(jnp.float32)[:, None] * frequency[None, :]
    angles = jnp.concatenate([angles, angles], axis=-1)
    return (jnp.cos(angles), jnp.sin(angles))

def rotate_half(values, cosine, sine):
    half_size = values.shape[-1] // 2
    turned = jnp.concatenate([-values[..., half_size:], values[..., :half_size]], axis=-1)
    return values * cosine + turned * sine

def head_path(projected, gain, cosine, sine, head_count):
    row_count = projected.shape[0]
    shaped = projected.reshape(row_count, head_count, -1)
    normed = rms_norm(shaped, gain)
    return rotate_half(normed, cosine[:, None, :], sine[:, None, :]).reshape(row_count, -1)

def head_attend(operands, positions, valid):
    queries, keys_here, values_here = operands
    scale = queries.shape[-1] ** (-0.5)
    raw_scores = jnp.einsum('tgd,sd->gts', queries, keys_here, precision=HIGHEST)
    allowed = valid[None, :] & (positions[None, :] <= positions[:, None])
    exp_scores = jnp.where(allowed[None], jnp.exp(low_back(raw_scores * scale)), 0.0)
    totals = lax.optimization_barrier(jnp.sum(exp_scores, axis=-1))
    accum = low_back(jnp.einsum('gts,sd->tgd', low(exp_scores), values_here, precision=HIGHEST))
    return accum / totals.T[:, :, None]

def layer(inputs, positions, valid, parameters):
    attn_gain, w_query, w_key, w_value, w_out, query_gain, key_gain, ffn_gain, w_gate, w_up, w_down = parameters
    head_size = query_gain.shape[0]
    query_heads = w_query.shape[1] // head_size
    key_heads = w_key.shape[1] // head_size
    group_size = query_heads // key_heads
    row_count = inputs.shape[0]
    cosine, sine = rotary_tables(positions, head_size)
    normed = low(rms_norm(inputs, attn_gain))
    queries = low(head_path(low_back(matmul(normed, w_query)), query_gain, cosine, sine, query_heads))
    keys_all = low(head_path(low_back(matmul(normed, w_key)), key_gain, cosine, sine, key_heads))
    values_all = low(low_back(matmul(normed, w_value)))
    queries = queries.reshape(row_count, key_heads, group_size, head_size).transpose(1, 0, 2, 3)
    keys_all = keys_all.reshape(row_count, key_heads, head_size).transpose(1, 0, 2)
    values_all = values_all.reshape(row_count, key_heads, head_size).transpose(1, 0, 2)
    mixed = lax.map(jax.checkpoint(lambda operands: head_attend(operands, positions, valid)), (queries, keys_all, values_all))
    mixed = low(mixed.transpose(1, 0, 2, 3).reshape(row_count, query_heads * head_size))
    hidden = inputs + low_back(matmul(mixed, w_out))
    normed_two = low(rms_norm(hidden, ffn_gain))
    gate = low_back(matmul(normed_two, w_gate))
    upper = low_back(matmul(normed_two, w_up))
    inner = low(jax.nn.silu(gate) * upper)
    return hidden + matmul(inner, w_down)

def reference(tokens, cotangent, lengths, deal, attn_gain, w_query, w_key, w_value, w_out, query_gain, key_gain, ffn_gain, w_gate, w_up, w_down):
    group_count = lengths.shape[0]
    slot_count = deal.shape[1] * BLK
    model_width = tokens.shape[1]
    positions = (deal[:, :, None] * BLK + jnp.arange(BLK, dtype=jnp.int32)[None, None, :]).reshape(group_count, slot_count)
    valid = positions < lengths[:, None]
    inputs = tokens.astype(jnp.float32).reshape(group_count, slot_count, model_width)
    parameters = tuple((item.astype(jnp.float32) for item in (attn_gain, w_query, w_key, w_value, w_out, query_gain, key_gain, ffn_gain, w_gate, w_up, w_down)))

    def forward(layer_input, layer_parameters):

        def one_group(operands):
            return layer(operands[0], operands[1], operands[2], layer_parameters)
        return lax.map(jax.checkpoint(one_group), (layer_input, positions, valid))
    result, pullback = jax.vjp(forward, inputs, parameters)
    seed_grad = cotangent.astype(jnp.float32).reshape(group_count, slot_count, model_width) * valid[:, :, None].astype(jnp.float32)
    grad_input, grad_params = pullback(seed_grad)
    return (result.reshape(group_count * slot_count, model_width).astype(jnp.bfloat16), grad_input.reshape(group_count * slot_count, model_width), grad_params[0], grad_params[1], grad_params[2], grad_params[3], grad_params[4], grad_params[5], grad_params[6], grad_params[7], grad_params[8], grad_params[9], grad_params[10])
```

```python
import functools
import math

import jax
import jax.numpy as jnp
from jax import lax
from jax.experimental import pallas as pl
from jax.experimental.pallas import tpu as pltpu
from jax.sharding import PartitionSpec as P

BLK = 128
EPS = 1e-06
THETA = 1000000.0
CTX = 4
TILE = 256


def _dot(a, b, dims):
    return lax.dot_general(a, b, (dims, ((), ())), preferred_element_type=jnp.float32)


def _forward_kernel(heads, scale, info, *refs):
    waves = refs[:-11]
    cos_ref, sin_ref, qg_ref, kg_ref, low_ref, mixed_ref, mlow_ref, rtot_ref, q_s, k_s, v_s = refs[-11:]
    hd = cos_ref.shape[1]
    rows = cos_ref.shape[0]
    wave_rows = rows // len(waves)
    factor = scale * math.log2(math.e)

    def prepare(block, wave_ref, base):
        local = pl.multiple_of(block * BLK, BLK)
        at = pl.multiple_of(base + block * BLK, BLK)
        here = pl.ds(at, BLK)
        cosine = cos_ref[here, :]
        sine = sin_ref[here, :]
        for h in range(heads + 1):
            u = wave_ref[pl.ds(local, BLK), h * hd : (h + 1) * hd]
            gain = qg_ref[...] if h < heads else kg_ref[...]
            n = u * lax.rsqrt(jnp.mean(u * u, axis=1, keepdims=True) + EPS) * gain
            o = (n * cosine + pltpu.roll(n, hd // 2, 1) * sine).astype(jnp.bfloat16)
            low_ref[here, h * hd : (h + 1) * hd] = o
            if h < heads:
                q_s[h, here, :] = o
            else:
                k_s[here, :] = o
        val = wave_ref[pl.ds(local, BLK), (heads + 1) * hd :].astype(jnp.bfloat16)
        low_ref[here, (heads + 1) * hd :] = val
        v_s[here, :] = val

    for w, wave_ref in enumerate(waves):

        @pl.loop(0, wave_rows // BLK)
        def _(block, wave_ref=wave_ref, base=w * wave_rows):
            prepare(block, wave_ref, base)

    length = info[rows // BLK]
    per = TILE // BLK

    def gather(ref, tile, *lead):
        parts = [
            ref[lead + (pl.ds(pl.multiple_of(info[tile * per + b] * BLK, BLK), BLK), slice(None))]
            for b in range(per)
        ]
        return jnp.concatenate(parts, axis=0)

    @pl.loop(0, rows // TILE)
    def _(i):
        query = jnp.concatenate([gather(q_s, i, h) for h in range(heads)], axis=0)
        full = jnp.minimum(i, length // TILE)

        def scores(j):
            return jnp.exp2(_dot(query, gather(k_s, j), ((1,), (1,))) * factor)

        def take(expo, j, acc, tot):
            part = expo[:, :hd]
            for b in range(1, TILE // hd):
                part = part + expo[:, b * hd : (b + 1) * hd]
            acc = acc + _dot(expo.astype(jnp.bfloat16), gather(v_s, j), ((1,), (0,)))
            return acc, tot + part

        def step(j, carry):
            return take(scores(j), j, *carry)

        zero = jnp.zeros((heads * TILE, hd), jnp.float32)
        acc, tot = lax.fori_loop(0, full, step, (zero, zero))
        expo = scores(full)
        qpos = i * TILE + lax.rem(lax.broadcasted_iota(jnp.int32, expo.shape, 0), TILE)
        kpos = full * TILE + lax.broadcasted_iota(jnp.int32, expo.shape, 1)
        expo = jnp.where((kpos <= qpos) & (kpos < length), expo, 0.0)
        acc, tot = take(expo, full, acc, tot)
        recip = 1.0 / jnp.sum(tot, axis=1, keepdims=True)
        mixed = acc * recip
        recip = jnp.broadcast_to(recip, mixed.shape)
        for h in range(heads):
            for b in range(per):
                at = pl.ds(pl.multiple_of(info[i * per + b] * BLK, BLK), BLK)
                cut = slice(h * TILE + b * BLK, h * TILE + (b + 1) * BLK)
                lanes = slice(h * hd, (h + 1) * hd)
                mixed_ref[at, lanes] = mixed[cut]
                mlow_ref[at, lanes] = mixed[cut].astype(jnp.bfloat16)
                rtot_ref[at, lanes] = recip[cut]


def attend_forward(info, waves, cosine, sine, query_gain, key_gain, heads):
    rows, hd = cosine.shape
    assert waves[0].shape[1] == (heads + 2) * hd
    width = heads * hd
    pairs = rows * rows // 2 * heads
    return pl.pallas_call(
        functools.partial(_forward_kernel, heads, hd**-0.5),
        out_shape=(
            jax.ShapeDtypeStruct((rows, (heads + 2) * hd), jnp.bfloat16),
            jax.ShapeDtypeStruct((rows, width), jnp.float32),
            jax.ShapeDtypeStruct((rows, width), jnp.bfloat16),
            jax.ShapeDtypeStruct((rows, width), jnp.float32),
        ),
        in_specs=[pl.BlockSpec(memory_space=pltpu.SMEM)]
        + [pl.BlockSpec(memory_space=pltpu.VMEM)] * (len(waves) + 4),
        out_specs=[pl.BlockSpec(memory_space=pltpu.VMEM)] * 4,
        scratch_shapes=[
            pltpu.VMEM((heads, rows, hd), jnp.bfloat16),
            pltpu.VMEM((rows, hd), jnp.bfloat16),
            pltpu.VMEM((rows, hd), jnp.bfloat16),
        ],
        compiler_params=pltpu.CompilerParams(vmem_limit_bytes=48 * 2**20),
        cost_estimate=pl.CostEstimate(
            flops=pairs * hd * 4, bytes_accessed=rows * hd * 60, transcendentals=pairs
        ),
        name="attend_forward",
    )(info, *waves, cosine, sine, query_gain, key_gain)


def _backward_kernel(heads, scale, info, *refs):
    count = (len(refs) - 13) // 2
    waves, gmixed = refs[:count], refs[count : 2 * count]
    (low_ref, mixed_ref, rtot_ref, cos_ref, sin_ref, qg_ref, kg_ref, out_ref, gain_ref, gacc_s, dq_s, dk_s, dv_s) = refs[
        2 * count :
    ]
    hd = cos_ref.shape[1]
    rows = cos_ref.shape[0]
    wave_rows = rows // count
    factor = scale * math.log2(math.e)
    length = info[rows // BLK]
    per = TILE // BLK

    dk_s[...] = jnp.zeros_like(dk_s)
    dv_s[...] = jnp.zeros_like(dv_s)
    gain_ref[...] = jnp.zeros_like(gain_ref)

    for w, g_ref in enumerate(gmixed):

        @pl.loop(0, wave_rows // BLK)
        def _(block, g_ref=g_ref, base=w * wave_rows):
            local = pl.ds(pl.multiple_of(block * BLK, BLK), BLK)
            at = pl.ds(pl.multiple_of(base + block * BLK, BLK), BLK)
            for h in range(heads):
                lanes = slice(h * hd, (h + 1) * hd)
                g = g_ref[local, lanes] * rtot_ref[at, lanes]
                gacc_s[h, at, :] = g.astype(jnp.bfloat16)
                dq_s[h, at, :] = g * mixed_ref[at, lanes]

    def spots(tile):
        return [pl.ds(pl.multiple_of(info[tile * per + b] * BLK, BLK), BLK) for b in range(per)]

    @pl.loop(0, pl.cdiv(length, TILE))
    def _(i):
        at = spots(i)
        query = jnp.concatenate(
            [low_ref[s, h * hd : (h + 1) * hd] for h in range(heads) for s in at], axis=0
        )
        gacc = jnp.concatenate([gacc_s[h, s, :] for h in range(heads) for s in at], axis=0)
        terms = jnp.concatenate([dq_s[h, s, :] for h in range(heads) for s in at], axis=0)
        shift = jnp.sum(terms.T, axis=0, keepdims=True)

        def tile(j, dq, masked):
            spot = spots(j)
            key = jnp.concatenate([low_ref[s, heads * hd : (heads + 1) * hd] for s in spot], axis=0)
            val = jnp.concatenate([low_ref[s, (heads + 1) * hd :] for s in spot], axis=0)
            expo = jnp.exp2(_dot(key, query, ((1,), (1,))) * factor)
            if masked:
                kpos = j * TILE + lax.broadcasted_iota(jnp.int32, expo.shape, 0)
                qpos = i * TILE + lax.rem(lax.broadcasted_iota(jnp.int32, expo.shape, 1), TILE)
                expo = jnp.where((kpos <= qpos) & (kpos < length), expo, 0.0)
            probs = _dot(val, gacc, ((1,), (1,)))
            ds = (expo * (probs - shift)).astype(jnp.bfloat16)
            dv = _dot(expo.astype(jnp.bfloat16), gacc, ((1,), (0,)))
            dk = _dot(ds, query, ((1,), (0,)))
            for b, s in enumerate(spot):
                dv_s[s, :] += dv[b * BLK : (b + 1) * BLK]
                dk_s[s, :] += dk[b * BLK : (b + 1) * BLK]
            return dq + _dot(ds, key, ((0,), (0,)))

        zero = jnp.zeros((heads * TILE, hd), jnp.float32)
        dq = lax.fori_loop(0, i, lambda j, dq: tile(j, dq, False), zero)
        dq = tile(i, dq, True) * scale
        for h in range(heads):
            for b, s in enumerate(at):
                dq_s[h, s, :] = dq[h * TILE + b * BLK : h * TILE + (b + 1) * BLK]

    def finish(wave_ref, block, base):
        local = pl.ds(pl.multiple_of(block * BLK, BLK), BLK)
        at = pl.ds(pl.multiple_of(base + block * BLK, BLK), BLK)
        cosine = cos_ref[at, :]
        sine = sin_ref[at, :]
        for h in range(heads + 1):
            lanes = slice(h * hd, (h + 1) * hd)
            u = wave_ref[local, lanes]
            r = lax.rsqrt(jnp.mean(u * u, axis=1, keepdims=True) + EPS)
            d = dq_s[h, at, :] if h < heads else dk_s[at, :] * scale
            dn = d * cosine - pltpu.roll(d, hd // 2, 1) * sine
            gain = qg_ref[...] if h < heads else kg_ref[...]
            hat = u * r
            row = 0 if h < heads else 1
            gain_ref[row : row + 1, :] += jnp.sum(dn * hat, axis=0, keepdims=True)
            dg = dn * gain
            du = r * (dg - hat * jnp.mean(dg * hat, axis=1, keepdims=True))
            out_ref[at, lanes] = du.astype(jnp.bfloat16)
        out_ref[at, (heads + 1) * hd :] = dv_s[at, :].astype(jnp.bfloat16)

    for b in range(rows // BLK):

        @pl.when(b * BLK >= pl.cdiv(length, TILE) * TILE)
        def _(b=b):
            at = pl.ds(pl.multiple_of(info[b] * BLK, BLK), BLK)
            for h in range(heads):
                dq_s[h, at, :] = jnp.zeros((BLK, hd), jnp.float32)

    for w, wave_ref in enumerate(waves):

        @pl.loop(0, wave_rows // BLK)
        def _(block, wave_ref=wave_ref, base=w * wave_rows):
            finish(wave_ref, block, base)


def attend_backward(info, waves, gmixed, low, mixed, rtot, cosine, sine, query_gain, key_gain, heads):
    rows, hd = cosine.shape
    pairs = rows * rows // 2 * heads
    return pl.pallas_call(
        functools.partial(_backward_kernel, heads, hd**-0.5),
        out_shape=(
            jax.ShapeDtypeStruct((rows, (heads + 2) * hd), jnp.bfloat16),
            jax.ShapeDtypeStruct((8, hd), jnp.float32),
        ),
        in_specs=[pl.BlockSpec(memory_space=pltpu.SMEM)]
        + [pl.BlockSpec(memory_space=pltpu.VMEM)] * (2 * len(waves) + 7),
        out_specs=[pl.BlockSpec(memory_space=pltpu.VMEM)] * 2,
        scratch_shapes=[
            pltpu.VMEM((heads, rows, hd), jnp.bfloat16),
            pltpu.VMEM((heads, rows, hd), jnp.float32),
            pltpu.VMEM((rows, hd), jnp.float32),
            pltpu.VMEM((rows, hd), jnp.float32),
        ],
        compiler_params=pltpu.CompilerParams(vmem_limit_bytes=48 * 2**20),
        cost_estimate=pl.CostEstimate(
            flops=pairs * hd * 10, bytes_accessed=rows * hd * 100, transcendentals=pairs
        ),
        name="attend_backward",
    )(info, *waves, *gmixed, low, mixed, rtot, cosine, sine, query_gain, key_gain)


def product(left, right):
    return jnp.dot(left, right, preferred_element_type=jnp.float32)


def left_transposed(left, right):
    return lax.dot_general(
        left, right, (((0,), (0,)), ((), ())), preferred_element_type=jnp.float32
    )


def right_transposed(left, right):
    return lax.dot_general(
        left, right, (((1,), (1,)), ((), ())), preferred_element_type=jnp.float32
    )


def low(values):
    return values.astype(jnp.bfloat16)


def wide(values):
    return values.astype(jnp.float32)


def across(values, bits):
    return lax.ppermute(values, "ctx", [(i, i ^ bits) for i in range(CTX)])


def other_core(values):
    return lax.ppermute(values, "tp", [(0, 1), (1, 0)])


def next_stage(values):
    count = lax.axis_size("fsdp")
    return lax.ppermute(values, "fsdp", [(i, (i - 1) % count) for i in range(count)])


def in_order(pieces, spot, axis):
    for bit in (1, 2):
        odd = (spot & bit) != 0
        pieces = [jnp.where(odd, pieces[j ^ bit], pieces[j]) for j in range(CTX)]
    return jnp.concatenate(pieces, axis=axis)


def gather_rows(own):
    half = own.shape[0] // 2
    own_other = other_core(own)
    by_x = across(own, 1)
    by_y = across(own, 2)
    x_other = other_core(by_x)
    y_other = other_core(by_y)
    far_top = across(by_x[:half], 2)
    far_bottom = across(by_y[half:], 1)
    far = jnp.concatenate([far_top, far_bottom], axis=0)
    far_other = other_core(far)
    return [
        jnp.concatenate(pair, axis=0)
        for pair in ((own, own_other), (by_x, x_other), (by_y, y_other), (far, far_other))
    ]


def scatter_rows(part):
    def over_cores(chip):
        mine, others = part(chip)
        return mine + wide(other_core(low(others)))

    far = low(over_cores(3))
    half = far.shape[0] // 2
    to_y = across(far[:half], 1)
    to_x = across(far[half:], 2)
    by_x = over_cores(1)
    by_x = low(jnp.concatenate([by_x[:half], by_x[half:] + wide(to_x)], axis=0))
    from_x = across(by_x, 1)
    by_y = over_cores(2)
    by_y = low(jnp.concatenate([by_y[:half] + wide(to_y), by_y[half:]], axis=0))
    from_y = across(by_y, 2)
    return over_cores(0) + wide(from_x) + wide(from_y)


def halves(left, right_of):
    half = left.shape[0] // 2
    return right_of(left[:half]), right_of(left[half:])


def deal_out(values, spot, size, axis):
    got = []
    for j in range(CTX):
        piece = [
            lax.dynamic_slice_in_dim(v, (spot ^ j) * n, n, axis) for v, n in zip(values, size)
        ]
        piece = jnp.concatenate(piece, axis=axis) if len(piece) > 1 else piece[0]
        got.append(across(piece, j) if j else piece)
    return got


def ring_gather(shard):
    pieces = [shard]
    for _ in range(lax.axis_size("fsdp") - 1):
        pieces.append(next_stage(pieces[-1]))
    return pieces


def ring_sum(chunk):
    count = lax.axis_size("fsdp")
    total = chunk(1 % count)
    for step in range(2, count + 1):
        total = chunk(step % count) + wide(next_stage(low(total)))
    return total


def turned(values, shift, count):
    width = values.shape[1]
    return lax.dynamic_slice_in_dim(
        jnp.concatenate([values, values], axis=1), shift * (width // count), width, 1
    )


def on_device(
    tokens,
    cotangent,
    lengths,
    deal,
    attn_gain,
    w_query,
    w_key,
    w_value,
    w_out,
    query_gain,
    key_gain,
    ffn_gain,
    w_gate,
    w_up,
    w_down,
):
    stage = lax.axis_index("fsdp")
    stages = lax.axis_size("fsdp")
    spot = lax.axis_index("ctx")
    core = lax.axis_index("tp")
    local_rows, width = tokens.shape
    head_size = query_gain.shape[0]
    rows = local_rows * CTX
    half_rows = local_rows // 2
    heads = w_query.shape[1] // head_size // CTX
    query_cols = heads * head_size
    units = w_gate.shape[1] // CTX
    chunk = width // stages
    shard = chunk // CTX

    attn_scale = wide(attn_gain)[:, None]
    feed_scale = wide(ffn_gain)[:, None]
    scaled = [low(wide(w) * attn_scale) for w in (w_query, w_key, w_value)]
    proj_shard = in_order(
        deal_out(scaled, spot, (query_cols, head_size, head_size), 1), spot, 0
    )
    proj_weight = jnp.concatenate(ring_gather(proj_shard), axis=0)
    out_shard = in_order(deal_out([w_out], spot, (query_cols,), 0), spot, 1)
    out_weight = jnp.concatenate(ring_gather(out_shard), axis=1)
    scaled = [low(wide(w) * feed_scale) for w in (w_gate, w_up)]
    feed_shard = in_order(deal_out(scaled, spot, (units, units), 1), spot, 0)
    feed_weight = jnp.concatenate(ring_gather(feed_shard), axis=0)
    down_shard = in_order(deal_out([w_down], spot, (units,), 0), spot, 1)
    down_weight = jnp.concatenate(ring_gather(down_shard), axis=1)

    per_half = half_rows // BLK
    order = jnp.arange(deal.shape[1], dtype=jnp.int32).reshape(CTX, 2, per_half)
    chips = jnp.arange(CTX, dtype=jnp.int32) ^ spot
    cores = jnp.arange(2, dtype=jnp.int32) ^ core
    order = ((chips[:, None] * 2 + cores[None, :])[:, :, None] * per_half + order[0, 0]).reshape(-1)
    blocks = jnp.sum(
        jnp.where(order[:, None] == jnp.arange(order.shape[0])[None, :], deal[0][None, :], 0), axis=1
    )
    spots = jnp.arange(order.shape[0], dtype=jnp.int32)
    where_is = jnp.sum(
        jnp.where(blocks[None, :] == spots[:, None], spots[None, :], 0), axis=1
    ).astype(jnp.int32)
    info = jnp.concatenate([where_is, lengths])
    positions = (blocks[:, None] * BLK + jnp.arange(BLK, dtype=jnp.int32)[None, :]).reshape(-1)
    frequency = THETA ** (-(jnp.arange(head_size // 2, dtype=jnp.float32) * 2.0 / head_size))
    angles = wide(positions)[:, None] * frequency[None, :]
    cosine, sine = jnp.cos(angles), jnp.sin(angles)
    cosine = jnp.concatenate([cosine, cosine], axis=1)
    sine = jnp.concatenate([-sine, sine], axis=1)
    query_scale = wide(query_gain)[None, :]
    key_scale = wide(key_gain)[None, :]

    own = lax.dynamic_slice_in_dim(tokens, core * half_rows, half_rows, 0)
    inputs = wide(turned(own, stage, stages))
    rstd = lax.rsqrt(jnp.mean(inputs * inputs, axis=1, keepdims=True) + EPS)
    hat = inputs * rstd
    normed = gather_rows(low(hat))
    projected = [product(n, proj_weight) for n in normed]
    qkv, mixed, mixed_low, recip = attend_forward(
        info, projected, cosine, sine, query_scale, key_scale, heads
    )

    def rows_of(values, chip):
        return values[chip * local_rows : (chip + 1) * local_rows]

    attn = scatter_rows(
        lambda chip: halves(rows_of(mixed_low, chip), lambda m: product(m, out_weight))
    )
    hidden = inputs + attn

    valid = positions[:half_rows] < lengths[0]
    seed = lax.dynamic_slice_in_dim(cotangent, core * half_rows, half_rows, 0)
    seed = jnp.where(valid[:, None], turned(seed, stage, stages), 0).astype(jnp.bfloat16)
    seeds = gather_rows(seed)
    rstd_two = lax.rsqrt(jnp.mean(hidden * hidden, axis=1, keepdims=True) + EPS)
    hat_two = hidden * rstd_two
    normed_two = gather_rows(low(hat_two))
    inner, grads = [], []
    for chip in range(CTX):
        gate_up = product(normed_two[chip], feed_weight)
        gate, upper = gate_up[:, :units], gate_up[:, units:]
        grad_inner = right_transposed(seeds[chip], down_weight)
        sigma = jax.nn.sigmoid(gate)
        silu = gate * sigma
        inner.append(low(silu * upper))
        grad_gate = grad_inner * upper * sigma * (1.0 + gate * (1.0 - sigma))
        grads.append(low(jnp.concatenate([grad_gate, grad_inner * silu], axis=1)))
    grad_normed_two = scatter_rows(
        lambda chip: halves(grads[chip], lambda g: right_transposed(g, feed_weight))
    )
    feed = scatter_rows(lambda chip: halves(inner[chip], lambda m: product(m, down_weight)))
    output_half = low(hidden + feed)
    grad_hat = grad_normed_two - hat_two * jnp.mean(
        grad_normed_two * hat_two, axis=1, keepdims=True
    )
    grad_hidden = wide(seed) + rstd_two * grad_hat
    grad_attn = gather_rows(low(grad_hidden))

    inner_all = jnp.concatenate(inner, axis=0)
    seed_all = jnp.concatenate(seeds, axis=0)
    grads_all = jnp.concatenate(grads, axis=0)
    normed_two_all = jnp.concatenate(normed_two, axis=0)
    grad_down = ring_sum(
        lambda k: left_transposed(inner_all, seed_all[:, k * chunk : (k + 1) * chunk])
    )
    grad_feed = ring_sum(
        lambda k: left_transposed(normed_two_all[:, k * chunk : (k + 1) * chunk], grads_all)
    )

    grad_mixed = [right_transposed(g, out_weight) for g in grad_attn]
    grad_proj, gain_sums = attend_backward(
        info, projected, grad_mixed, qkv, mixed, recip, cosine, sine, query_scale, key_scale, heads
    )
    grad_normed = scatter_rows(
        lambda chip: halves(
            rows_of(grad_proj, chip), lambda g: right_transposed(g, proj_weight)
        )
    )
    grad_attn_all = jnp.concatenate(grad_attn, axis=0)
    normed_all = jnp.concatenate(normed, axis=0)
    grad_out = ring_sum(
        lambda k: left_transposed(mixed_low, grad_attn_all[:, k * chunk : (k + 1) * chunk])
    )
    grad_project = ring_sum(
        lambda k: left_transposed(normed_all[:, k * chunk : (k + 1) * chunk], grad_proj)
    )
    grad_hat = grad_normed - hat * jnp.mean(grad_normed * hat, axis=1, keepdims=True)
    grad_tokens_half = grad_hidden + rstd * grad_hat

    def whole_rows(values):
        values = turned(values, (stages - stage) % stages, stages)
        other = other_core(values)
        first = core == 0
        return jnp.concatenate(
            [jnp.where(first, values, other), jnp.where(first, other, values)], axis=0
        )

    def dealt_rows(values):
        values = low(values)
        got = [
            lax.dynamic_slice_in_dim(values, (spot ^ j) * shard, shard, 0) for j in range(CTX)
        ]
        return [across(v, j) if j else v for j, v in enumerate(got)]

    def dealt_cols(values):
        values = low(values)
        got = [
            lax.dynamic_slice_in_dim(values, (spot ^ j) * shard, shard, 1) for j in range(CTX)
        ]
        return wide(in_order([across(v, j) if j else v for j, v in enumerate(got)], spot, 0))

    def cut(pieces, start, size):
        return wide(in_order([p[:, start : start + size] for p in pieces], spot, 1))

    feed_pieces = dealt_rows(grad_feed)
    grad_gate_w = cut(feed_pieces, 0, units)
    grad_up_w = cut(feed_pieces, units, units)
    proj_pieces = dealt_rows(grad_project)
    grad_query_w = cut(proj_pieces, 0, query_cols)
    grad_key_w = cut(proj_pieces, query_cols, head_size)
    grad_value_w = cut(proj_pieces, query_cols + head_size, head_size)

    def gain_part(pairs):
        return sum(jnp.sum(wide(w) * g, axis=1) for w, g in pairs)

    feed_gain = gain_part(((w_gate, grad_gate_w), (w_up, grad_up_w)))
    norm_gain = gain_part(((w_query, grad_query_w), (w_key, grad_key_w), (w_value, grad_value_w)))
    feed_gain = feed_gain + other_core(feed_gain)
    norm_gain = norm_gain + other_core(norm_gain)
    gain_sums = gain_sums + other_core(gain_sums)
    for bit in (1, 2):
        gain_sums = gain_sums + across(gain_sums, bit)
    term = gain_sums
    for _ in range(stages - 1):
        term = next_stage(term)
        gain_sums = gain_sums + term
    return (
        whole_rows(output_half),
        whole_rows(grad_tokens_half),
        norm_gain,
        grad_query_w * attn_scale,
        grad_key_w * attn_scale,
        grad_value_w * attn_scale,
        dealt_cols(grad_out),
        gain_sums[0],
        gain_sums[1],
        feed_gain,
        grad_gate_w * feed_scale,
        grad_up_w * feed_scale,
        dealt_cols(grad_down),
    )


def solution(mesh):
    return jax.shard_map(
        on_device,
        mesh=mesh,
        in_specs=(
            P(("fsdp", "ctx"), None),
            P(("fsdp", "ctx"), None),
            P("fsdp"),
            P("fsdp", None),
            P(("fsdp", "ctx")),
            P(("fsdp", "ctx"), "tp"),
            P(("fsdp", "ctx"), "tp"),
            P(("fsdp", "ctx"), "tp"),
            P("tp", ("fsdp", "ctx")),
            P(),
            P(),
            P(("fsdp", "ctx")),
            P(("fsdp", "ctx"), "tp"),
            P(("fsdp", "ctx"), "tp"),
            P("tp", ("fsdp", "ctx")),
        ),
        out_specs=(
            P(("fsdp", "ctx"), None),
            P(("fsdp", "ctx"), None),
            P(("fsdp", "ctx")),
            P(("fsdp", "ctx"), "tp"),
            P(("fsdp", "ctx"), "tp"),
            P(("fsdp", "ctx"), "tp"),
            P("tp", ("fsdp", "ctx")),
            P(),
            P(),
            P(("fsdp", "ctx")),
            P(("fsdp", "ctx"), "tp"),
            P(("fsdp", "ctx"), "tp"),
            P("tp", ("fsdp", "ctx")),
        ),
        check_vma=False,
    )
```

```python
import functools
import math

import jax
import jax.numpy as jnp
from jax import lax
from jax.experimental import pallas as pl
from jax.experimental.pallas import tpu as pltpu
from jax.sharding import PartitionSpec as P

BLK = 128
EPS = 1e-06
THETA = 1000000.0
CTX = 4
LIMIT = 56 * 2**20
TILE = 256


def _dot(a, b, dims):
    return lax.dot_general(a, b, (dims, ((), ())), preferred_element_type=jnp.float32)


def _starts(pieces):
    at, starts = 0, []
    for piece in pieces:
        starts.append(at)
        at += piece.shape[0]
    return starts


def _whole(count):
    return [pl.BlockSpec(memory_space=pltpu.VMEM)] * count


def _forward_kernel(heads, scale, info, *refs):
    pieces = refs[:-13]
    (weight_ref, cos_ref, sin_ref, qg_ref, kg_ref, proj_ref, low_ref, mixed_ref, mlow_ref, rtot_ref, q_s, k_s, v_s) = refs[
        -13:
    ]
    hd = cos_ref.shape[1]
    rows = cos_ref.shape[0]
    cols = proj_ref.shape[1]
    factor = scale * math.log2(math.e)

    for piece, start in zip(pieces, _starts(pieces)):
        proj_ref[start : start + piece.shape[0], :] = _dot(
            piece[...], weight_ref[:, :cols], ((1,), (0,))
        )

    @pl.loop(0, rows // BLK)
    def _(block):
        here = pl.ds(pl.multiple_of(block * BLK, BLK), BLK)
        cosine = cos_ref[here, :]
        sine = sin_ref[here, :]
        for h in range(heads + 1):
            u = proj_ref[here, h * hd : (h + 1) * hd]
            gain = qg_ref[...] if h < heads else kg_ref[...]
            n = u * lax.rsqrt(jnp.mean(u * u, axis=1, keepdims=True) + EPS) * gain
            o = (n * cosine + pltpu.roll(n, hd // 2, 1) * sine).astype(jnp.bfloat16)
            low_ref[here, h * hd : (h + 1) * hd] = o
            if h < heads:
                q_s[h, here, :] = o
            else:
                k_s[here, :] = o
        val = proj_ref[here, (heads + 1) * hd :].astype(jnp.bfloat16)
        low_ref[here, (heads + 1) * hd :] = val
        v_s[here, :] = val

    length = info[rows // BLK]
    per = TILE // BLK

    def gather(ref, tile, *lead):
        parts = [
            ref[lead + (pl.ds(pl.multiple_of(info[tile * per + b] * BLK, BLK), BLK), slice(None))]
            for b in range(per)
        ]
        return jnp.concatenate(parts, axis=0)

    @pl.loop(0, rows // TILE)
    def _(i):
        query = jnp.concatenate([gather(q_s, i, h) for h in range(heads)], axis=0)
        full = jnp.minimum(i, length // TILE)

        def scores(j):
            return jnp.exp2(_dot(query, gather(k_s, j), ((1,), (1,))) * factor)

        def take(expo, j, acc, tot):
            part = expo[:, :hd]
            for b in range(1, TILE // hd):
                part = part + expo[:, b * hd : (b + 1) * hd]
            acc = acc + _dot(expo.astype(jnp.bfloat16), gather(v_s, j), ((1,), (0,)))
            return acc, tot + part

        def step(j, carry):
            return take(scores(j), j, *carry)

        zero = jnp.zeros((heads * TILE, hd), jnp.float32)
        acc, tot = lax.fori_loop(0, full, step, (zero, zero))
        expo = scores(full)
        qpos = i * TILE + lax.rem(lax.broadcasted_iota(jnp.int32, expo.shape, 0), TILE)
        kpos = full * TILE + lax.broadcasted_iota(jnp.int32, expo.shape, 1)
        expo = jnp.where((kpos <= qpos) & (kpos < length), expo, 0.0)
        acc, tot = take(expo, full, acc, tot)
        recip = 1.0 / jnp.sum(tot, axis=1, keepdims=True)
        mixed = acc * recip
        recip = jnp.broadcast_to(recip, mixed.shape)
        for h in range(heads):
            for b in range(per):
                at = pl.ds(pl.multiple_of(info[i * per + b] * BLK, BLK), BLK)
                cut = slice(h * TILE + b * BLK, h * TILE + (b + 1) * BLK)
                lanes = slice(h * hd, (h + 1) * hd)
                mixed_ref[at, lanes] = mixed[cut]
                mlow_ref[at, lanes] = mixed[cut].astype(jnp.bfloat16)
                rtot_ref[at, lanes] = recip[cut]


def attend_forward(info, pieces, weight, cosine, sine, query_gain, key_gain, heads):
    rows, hd = cosine.shape
    cols = (heads + 2) * hd
    width = heads * hd
    pairs = rows * rows // 2 * heads
    return pl.pallas_call(
        functools.partial(_forward_kernel, heads, hd**-0.5),
        out_shape=(
            jax.ShapeDtypeStruct((rows, cols), jnp.float32),
            jax.ShapeDtypeStruct((rows, cols), jnp.bfloat16),
            jax.ShapeDtypeStruct((rows, width), jnp.float32),
            jax.ShapeDtypeStruct((rows, width), jnp.bfloat16),
            jax.ShapeDtypeStruct((rows, width), jnp.float32),
        ),
        in_specs=[pl.BlockSpec(memory_space=pltpu.SMEM)] + _whole(len(pieces) + 5),
        out_specs=_whole(5),
        scratch_shapes=[
            pltpu.VMEM((heads, rows, hd), jnp.bfloat16),
            pltpu.VMEM((rows, hd), jnp.bfloat16),
            pltpu.VMEM((rows, hd), jnp.bfloat16),
        ],
        compiler_params=pltpu.CompilerParams(vmem_limit_bytes=LIMIT),
        cost_estimate=pl.CostEstimate(
            flops=pairs * hd * 4 + 2 * rows * cols * weight.shape[0],
            bytes_accessed=rows * hd * 100,
            transcendentals=pairs,
        ),
        name="attend_forward",
    )(info, *pieces, weight, cosine, sine, query_gain, key_gain)


def _backward_kernel(heads, scale, info, *refs):
    pieces = refs[:-15]
    (weight_ref, proj_ref, low_ref, mixed_ref, rtot_ref, cos_ref, sin_ref, qg_ref, kg_ref, out_ref, gain_ref, gacc_s, dq_s, dk_s, dv_s) = refs[
        -15:
    ]
    hd = cos_ref.shape[1]
    rows = cos_ref.shape[0]
    factor = scale * math.log2(math.e)
    length = info[rows // BLK]
    per = TILE // BLK
    cols = (heads + 2) * hd

    dk_s[...] = jnp.zeros_like(dk_s)
    dv_s[...] = jnp.zeros_like(dv_s)
    gain_ref[...] = jnp.zeros_like(gain_ref)

    for piece, start in zip(pieces, _starts(pieces)):
        grad = _dot(piece[...], weight_ref[:, cols:], ((1,), (0,)))
        at = slice(start, start + piece.shape[0])
        for h in range(heads):
            lanes = slice(h * hd, (h + 1) * hd)
            g = grad[:, lanes] * rtot_ref[at, lanes]
            gacc_s[h, at, :] = g.astype(jnp.bfloat16)
            dq_s[h, at, :] = g * mixed_ref[at, lanes]

    def spots(tile):
        return [pl.ds(pl.multiple_of(info[tile * per + b] * BLK, BLK), BLK) for b in range(per)]

    @pl.loop(0, pl.cdiv(length, TILE))
    def _(i):
        at = spots(i)
        query = jnp.concatenate(
            [low_ref[s, h * hd : (h + 1) * hd] for h in range(heads) for s in at], axis=0
        )
        gacc = jnp.concatenate([gacc_s[h, s, :] for h in range(heads) for s in at], axis=0)
        terms = jnp.concatenate([dq_s[h, s, :] for h in range(heads) for s in at], axis=0)
        shift = jnp.sum(terms.T, axis=0, keepdims=True)

        def tile(j, dq, masked):
            spot = spots(j)
            key = jnp.concatenate([low_ref[s, heads * hd : (heads + 1) * hd] for s in spot], axis=0)
            val = jnp.concatenate([low_ref[s, (heads + 1) * hd :] for s in spot], axis=0)
            expo = jnp.exp2(_dot(key, query, ((1,), (1,))) * factor)
            if masked:
                kpos = j * TILE + lax.broadcasted_iota(jnp.int32, expo.shape, 0)
                qpos = i * TILE + lax.rem(lax.broadcasted_iota(jnp.int32, expo.shape, 1), TILE)
                expo = jnp.where((kpos <= qpos) & (kpos < length), expo, 0.0)
            probs = _dot(val, gacc, ((1,), (1,)))
            ds = (expo * (probs - shift)).astype(jnp.bfloat16)
            dv = _dot(expo.astype(jnp.bfloat16), gacc, ((1,), (0,)))
            dk = _dot(ds, query, ((1,), (0,)))
            for b, s in enumerate(spot):
                dv_s[s, :] += dv[b * BLK : (b + 1) * BLK]
                dk_s[s, :] += dk[b * BLK : (b + 1) * BLK]
            return dq + _dot(ds, key, ((0,), (0,)))

        zero = jnp.zeros((heads * TILE, hd), jnp.float32)
        dq = lax.fori_loop(0, i, lambda j, dq: tile(j, dq, False), zero)
        dq = tile(i, dq, True) * scale
        for h in range(heads):
            for b, s in enumerate(at):
                dq_s[h, s, :] = dq[h * TILE + b * BLK : h * TILE + (b + 1) * BLK]

    def finish(block):
        at = pl.ds(pl.multiple_of(block * BLK, BLK), BLK)
        cosine = cos_ref[at, :]
        sine = sin_ref[at, :]
        for h in range(heads + 1):
            lanes = slice(h * hd, (h + 1) * hd)
            u = proj_ref[at, lanes]
            r = lax.rsqrt(jnp.mean(u * u, axis=1, keepdims=True) + EPS)
            d = dq_s[h, at, :] if h < heads else dk_s[at, :] * scale
            dn = d * cosine - pltpu.roll(d, hd // 2, 1) * sine
            gain = qg_ref[...] if h < heads else kg_ref[...]
            hat = u * r
            row = 0 if h < heads else 1
            gain_ref[row : row + 1, :] += jnp.sum(dn * hat, axis=0, keepdims=True)
            dg = dn * gain
            du = r * (dg - hat * jnp.mean(dg * hat, axis=1, keepdims=True))
            out_ref[at, lanes] = du.astype(jnp.bfloat16)
        out_ref[at, (heads + 1) * hd :] = dv_s[at, :].astype(jnp.bfloat16)

    for b in range(rows // BLK):

        @pl.when(b * BLK >= pl.cdiv(length, TILE) * TILE)
        def _(b=b):
            at = pl.ds(pl.multiple_of(info[b] * BLK, BLK), BLK)
            for h in range(heads):
                dq_s[h, at, :] = jnp.zeros((BLK, hd), jnp.float32)

    @pl.loop(0, rows // BLK)
    def _(block):
        finish(block)


def attend_backward(
    info, pieces, weight, proj, low, mixed, rtot, cosine, sine, query_gain, key_gain, heads
):
    rows, hd = cosine.shape
    pairs = rows * rows // 2 * heads
    return pl.pallas_call(
        functools.partial(_backward_kernel, heads, hd**-0.5),
        out_shape=(
            jax.ShapeDtypeStruct((rows, (heads + 2) * hd), jnp.bfloat16),
            jax.ShapeDtypeStruct((8, hd), jnp.float32),
        ),
        in_specs=[pl.BlockSpec(memory_space=pltpu.SMEM)] + _whole(len(pieces) + 9),
        out_specs=_whole(2),
        scratch_shapes=[
            pltpu.VMEM((heads, rows, hd), jnp.bfloat16),
            pltpu.VMEM((heads, rows, hd), jnp.float32),
            pltpu.VMEM((rows, hd), jnp.float32),
            pltpu.VMEM((rows, hd), jnp.float32),
        ],
        compiler_params=pltpu.CompilerParams(vmem_limit_bytes=LIMIT),
        cost_estimate=pl.CostEstimate(
            flops=pairs * hd * 10 + 2 * rows * heads * hd * weight.shape[0],
            bytes_accessed=rows * hd * 140,
            transcendentals=pairs,
        ),
        name="attend_backward",
    )(info, *pieces, weight, proj, low, mixed, rtot, cosine, sine, query_gain, key_gain)


def _expand_kernel(counts, *refs):
    groups = []
    for count in counts:
        groups.append(refs[:count])
        refs = refs[count:]
    gate_w, up_w = refs[:2]
    slope_ref, silu_ref, inner_ref = refs[-3:]
    for row, pieces in enumerate(groups):

        @pl.when(pl.program_id(0) == row)
        def _(pieces=pieces):
            for piece, start in zip(pieces, _starts(pieces)):
                at = slice(start, start + piece.shape[0])
                gate = _dot(piece[...], gate_w[...], ((1,), (0,)))
                upper = _dot(piece[...], up_w[...], ((1,), (0,)))
                sigma = 1.0 / (1.0 + jnp.exp(-gate))
                silu = gate * sigma
                slope_ref[at, :] = upper * sigma * (1.0 + gate - silu)
                silu_ref[at, :] = silu
                inner_ref[at, :] = (silu * upper).astype(jnp.bfloat16)


def feed_expand(groups, first, weight, rows, filled=(), step=256):
    size = sum(p.shape[0] for p in groups[0])
    width, units = weight.shape[0], weight.shape[1] // 2
    steps = units // step
    pieces = [p for group in groups for p in group]
    tile = pl.BlockSpec((size, step), lambda r, n: (r + first, n))
    done = size * len(groups)
    return pl.pallas_call(
        functools.partial(_expand_kernel, [len(group) for group in groups]),
        grid=(len(groups), steps),
        out_shape=(
            jax.ShapeDtypeStruct((rows, units), jnp.float32),
            jax.ShapeDtypeStruct((rows, units), jnp.float32),
            jax.ShapeDtypeStruct((rows, units), jnp.bfloat16),
        ),
        in_specs=[
            pl.BlockSpec(p.shape, lambda r, n: (0, 0), pipeline_mode=pl.Buffered(1)) for p in pieces
        ]
        + [
            pl.BlockSpec((width, step), lambda r, n: (0, n)),
            pl.BlockSpec((width, step), lambda r, n: (0, n + steps)),
        ]
        + [pl.BlockSpec(memory_space=pl.ANY)] * len(filled),
        out_specs=(tile, tile, tile),
        input_output_aliases={len(pieces) + 2 + i: i for i in range(len(filled))},
        compiler_params=pltpu.CompilerParams(vmem_limit_bytes=LIMIT),
        cost_estimate=pl.CostEstimate(
            flops=4 * done * width * units,
            bytes_accessed=done * width * 2 + width * units * 4 + done * units * 10,
            transcendentals=done * units,
        ),
        name="feed_expand",
    )(*pieces, weight, weight, *filled)


def _shrink_kernel(count, *refs):
    pieces = refs[:count]
    weight, slope_ref, silu_ref, dgate_ref, dup_ref = refs[count:]
    for piece, start in zip(pieces, _starts(pieces)):
        at = slice(start, start + piece.shape[0])
        grad = _dot(piece[...], weight[...], ((1,), (0,)))
        dgate_ref[at, :] = (grad * slope_ref[at, :]).astype(jnp.bfloat16)
        dup_ref[at, :] = (grad * silu_ref[at, :]).astype(jnp.bfloat16)


def feed_back(pieces, weight, slope, silu, step=256):
    rows = sum(p.shape[0] for p in pieces)
    width, units = weight.shape
    tile = pl.BlockSpec((rows, step), lambda n: (0, n))
    return pl.pallas_call(
        functools.partial(_shrink_kernel, len(pieces)),
        grid=(units // step,),
        out_shape=(jax.ShapeDtypeStruct((rows, units), jnp.bfloat16),) * 2,
        in_specs=[pl.BlockSpec(p.shape, lambda n: (0, 0), pipeline_mode=pl.Buffered(1)) for p in pieces]
        + [pl.BlockSpec((width, step), lambda n: (0, n)), tile, tile],
        out_specs=(tile, tile),
        compiler_params=pltpu.CompilerParams(vmem_limit_bytes=LIMIT),
        cost_estimate=pl.CostEstimate(
            flops=2 * rows * width * units,
            bytes_accessed=rows * width * 2 + width * units * 2 + rows * units * 12,
            transcendentals=0,
        ),
        name="feed_back",
    )(*pieces, weight, slope, silu)


def _terms_kernel(groups, *refs):
    out_ref, hold_s = refs[-2:]
    refs = refs[:-2]
    column = 0
    for count, sides in groups:
        pieces, others, refs = refs[:count], refs[count : count + sides], refs[count + sides :]
        for piece, start in zip(pieces, _starts(pieces)):
            hold_s[start : start + piece.shape[0], :] = piece[...]
        for other in others:
            size = other.shape[1]
            out_ref[:, column : column + size] = _dot(
                hold_s[...], other[...], ((0,), (0,))
            ).astype(jnp.bfloat16)
            column += size


def weight_terms(groups, step=256):
    width = groups[0][0][0].shape[1]
    rows = groups[0][1][0].shape[0]
    specs, values = [], []
    for pieces, others in groups:
        specs += [pl.BlockSpec((p.shape[0], step), lambda n: (0, n)) for p in pieces]
        specs += [pl.BlockSpec(o.shape, lambda n: (0, 0), pipeline_mode=pl.Buffered(1)) for o in others]
        values += list(pieces) + list(others)
    total = sum(o.shape[1] for _, others in groups for o in others)
    return pl.pallas_call(
        functools.partial(_terms_kernel, [(len(p), len(o)) for p, o in groups]),
        grid=(width // step,),
        out_shape=jax.ShapeDtypeStruct((width, total), jnp.bfloat16),
        in_specs=specs,
        out_specs=pl.BlockSpec((step, total), lambda n: (n, 0)),
        scratch_shapes=[pltpu.VMEM((rows, step), jnp.bfloat16)],
        compiler_params=pltpu.CompilerParams(vmem_limit_bytes=LIMIT),
        cost_estimate=pl.CostEstimate(
            flops=2 * rows * width * total,
            bytes_accessed=sum(v.size * 2 for v in values) + width * total * 2,
            transcendentals=0,
        ),
        name="weight_terms",
    )(*values)


def _rows_kernel(sides, blocks, arrived, cuts, *refs):
    lefts, refs = refs[: sides * blocks], refs[sides * blocks :]
    weight, refs = refs[0], refs[1:]
    there, outs = (refs[0], refs[1:]) if arrived else (None, refs)
    size = lefts[0].shape[0]
    at = 0
    for block in range(blocks):
        column, total = 0, None
        for side in range(sides):
            left = lefts[side * blocks + block]
            depth = left.shape[1]
            term = _dot(left[...], weight[:, column : column + depth], ((1,), (1,)))
            total = term if total is None else total + term
            column += depth
        if arrived:
            total = total + there[block * size : (block + 1) * size, :].astype(jnp.float32)
        row = 0
        while row < size:
            out = outs[cuts[at][0]]
            first, length = cuts[at][1], cuts[at][2]
            out[first : first + length, :] = total[row : row + length].astype(out.dtype)
            row += length
            at += 1


def rows_product(lefts, weight, column, picks, outs, cuts, there=None, size=256, step=512):
    width = weight.shape[0]
    depth = sum(v.shape[1] for v in lefts)
    specs = [
        pl.BlockSpec((size, v.shape[1]), lambda n, p=p: (p, 0), pipeline_mode=pl.Buffered(1))
        for v in lefts
        for p in picks
    ]
    specs.append(pl.BlockSpec((step, depth), lambda n: (n, column)))
    values = [v for v in lefts for _ in picks] + [weight]
    if there is not None:
        specs.append(pl.BlockSpec((there.shape[0], step), lambda n: (0, n)))
        values.append(there)
    rows = size * len(picks)
    return pl.pallas_call(
        functools.partial(_rows_kernel, len(lefts), len(picks), there is not None, cuts),
        grid=(width // step,),
        out_shape=[jax.ShapeDtypeStruct((r, width), t) for r, t in outs],
        in_specs=specs,
        out_specs=[pl.BlockSpec((r, step), lambda n: (0, n)) for r, _ in outs],
        compiler_params=pltpu.CompilerParams(vmem_limit_bytes=LIMIT),
        cost_estimate=pl.CostEstimate(
            flops=2 * rows * width * depth,
            bytes_accessed=rows * depth * 2 + width * depth * 2 + rows * width * 6,
            transcendentals=0,
        ),
        name="rows_product",
    )(*values)


def _settle_kernel(mode, *refs):
    total_ref, x_top, x_bottom, y_top, y_bottom = refs[:5]
    rest = refs[5:]
    rows = total_ref.shape[0]
    step = 32
    for start in range(0, rows, step):
        here = slice(start, start + step)
        upper = start < rows // 2
        there = here if upper else slice(start - rows // 2, start - rows // 2 + step)
        by_x, by_y = (x_top, y_top) if upper else (x_bottom, y_bottom)
        total = total_ref[here, :] + by_x[there, :].astype(jnp.float32) + by_y[there, :].astype(jnp.float32)
        if mode == "add":
            base_ref, out_ref = rest
            out_ref[here, :] = (base_ref[here, :] + total).astype(out_ref.dtype)
        elif mode == "norm":
            base_ref, out_ref, hat_ref = rest
            hidden = base_ref[here, :].astype(jnp.float32) + total
            out_ref[here, :] = hidden
            rstd = lax.rsqrt(jnp.mean(hidden * hidden, axis=1, keepdims=True) + EPS)
            hat_ref[here, :] = (hidden * rstd).astype(jnp.bfloat16)
        else:
            source_ref, base_ref = rest[:2]
            source = source_ref[here, :].astype(jnp.float32)
            rstd = lax.rsqrt(jnp.mean(source * source, axis=1, keepdims=True) + EPS)
            hat = source * rstd
            grad = total - hat * jnp.mean(total * hat, axis=1, keepdims=True)
            out = base_ref[here, :].astype(jnp.float32) + rstd * grad
            rest[2][here, :] = out
            if len(rest) > 3:
                rest[3][here, :] = out.astype(jnp.bfloat16)


def settle(mode, sums, others, types):
    rows, width = sums[0].shape
    return pl.pallas_call(
        functools.partial(_settle_kernel, mode),
        out_shape=[jax.ShapeDtypeStruct((rows, width), t) for t in types],
        in_specs=_whole(5 + len(others)),
        out_specs=_whole(len(types)),
        compiler_params=pltpu.CompilerParams(vmem_limit_bytes=LIMIT),
        cost_estimate=pl.CostEstimate(
            flops=rows * width * 10, bytes_accessed=rows * width * 20, transcendentals=rows
        ),
        name="settle",
    )(*sums, *others)


def low(values):
    return values.astype(jnp.bfloat16)


def wide(values):
    return values.astype(jnp.float32)


def after(values, *others):
    return lax.optimization_barrier((values,) + others)[0]


def across(values, bits):
    return lax.ppermute(values, "ctx", [(i, i ^ bits) for i in range(CTX)])


def other_core(values):
    return lax.ppermute(values, "tp", [(0, 1), (1, 0)])


def in_order(pieces, spot, axis):
    for bit in (1, 2):
        odd = (spot & bit) != 0
        pieces = [jnp.where(odd, pieces[j ^ bit], pieces[j]) for j in range(CTX)]
    return jnp.concatenate(pieces, axis=axis)


def gather_near(own):
    return other_core(own), across(own, 1), across(own, 2)


def gather_far(by_x, by_y):
    half = by_x.shape[0] // 2
    return other_core(by_x), other_core(by_y), across(by_x[:half], 2), across(by_y[half:], 1)


def gather_rows(own, beside=()):
    own_other, by_x, by_y = gather_near(own)
    by_x, by_y = after((by_x, by_y), beside)
    x_other, y_other, far_top, far_bottom = gather_far(by_x, by_y)
    far = [far_top, far_bottom, other_core(far_top), other_core(far_bottom)]
    return [own, own_other, by_x, x_other, by_y, y_other] + far


def scatter_rows(lefts, weight, column, beside=()):
    size = lefts[0].shape[0] // (2 * CTX)
    half = size // 2
    far_there = rows_product(lefts, weight, column, (7,), [(size, jnp.bfloat16)], [(0, 0, size)])[0]
    rest_there = rows_product(
        lefts,
        after(weight, far_there),
        column,
        (1, 3, 5),
        [(3 * size, jnp.bfloat16)],
        [(0, i * size, size) for i in range(3)],
    )[0]
    far_there = after(other_core(far_there), rest_there)
    rest_there = other_core(rest_there)
    far_top, far_bottom = rows_product(
        lefts,
        weight,
        column,
        (6,),
        [(half, jnp.bfloat16)] * 2,
        [(0, 0, half), (1, 0, half)],
        far_there,
    )
    far_top, far_bottom = after((far_top, far_bottom), beside)
    to_y = across(far_top, 1)
    to_x = across(far_bottom, 2)
    own, x_top, x_bottom, y_top, y_bottom = rows_product(
        lefts,
        after(weight, far_top),
        column,
        (0, 2, 4),
        [(size, jnp.float32)]
        + [(half, t) for t in (jnp.bfloat16, jnp.float32, jnp.float32, jnp.bfloat16)],
        [(0, 0, size)] + [(i, 0, half) for i in range(1, 5)],
        rest_there,
    )
    return [own, across(x_top, 1), across(y_bottom, 2), to_x, to_y, x_bottom, y_top], far_top


def scatter_end(parts, beside=()):
    own, from_x_top, from_y_bottom, to_x, to_y, x_bottom, y_top = parts
    to_x, to_y = after((to_x, to_y), own, beside)
    x_bottom = low(x_bottom + wide(to_x))
    y_top = low(y_top + wide(to_y))
    return [own, from_x_top, across(x_bottom, 1), across(y_top, 2), from_y_bottom], (x_bottom, y_top)


def deal_out(values, spot, size, axis):
    got = []
    for j in range(CTX):
        piece = [
            lax.dynamic_slice_in_dim(v, (spot ^ j) * n, n, axis) for v, n in zip(values, size)
        ]
        piece = jnp.concatenate(piece, axis=axis) if len(piece) > 1 else piece[0]
        got.append(across(piece, j) if j else piece)
    return got


def gather_stages(shard):
    return lax.all_gather(shard, "fsdp", axis=0, tiled=True)


def sum_stages(values):
    return lax.psum_scatter(values, "fsdp", scatter_dimension=0, tiled=True)


def on_device(
    tokens,
    cotangent,
    lengths,
    deal,
    attn_gain,
    w_query,
    w_key,
    w_value,
    w_out,
    query_gain,
    key_gain,
    ffn_gain,
    w_gate,
    w_up,
    w_down,
):
    stages = lax.axis_size("fsdp")
    spot = lax.axis_index("ctx")
    core = lax.axis_index("tp")
    local_rows, width = tokens.shape
    head_size = query_gain.shape[0]
    half_rows = local_rows // 2
    heads = w_query.shape[1] // head_size // CTX
    query_cols = heads * head_size
    proj_cols = query_cols + 2 * head_size
    units = w_gate.shape[1] // CTX
    shard = width // stages // CTX

    def dealt_rows(values):
        got = [
            lax.dynamic_slice_in_dim(values, (spot ^ j) * shard, shard, 0) for j in range(CTX)
        ]
        return [across(v, j) if j else v for j, v in enumerate(got)]

    attn_scale = wide(attn_gain)[:, None]
    feed_scale = wide(ffn_gain)[:, None]
    scaled = [low(wide(w) * attn_scale) for w in (w_query, w_key, w_value)]
    dealt = deal_out(scaled + [w_out.T], spot, (query_cols, head_size, head_size, query_cols), 1)
    attn_weight = gather_stages(in_order(dealt, spot, 0))

    per_half = half_rows // BLK
    order = jnp.arange(deal.shape[1], dtype=jnp.int32).reshape(CTX, 2, per_half)
    chips = jnp.arange(CTX, dtype=jnp.int32) ^ spot
    cores = jnp.arange(2, dtype=jnp.int32) ^ core
    order = ((chips[:, None] * 2 + cores[None, :])[:, :, None] * per_half + order[0, 0]).reshape(-1)
    blocks = jnp.sum(
        jnp.where(order[:, None] == jnp.arange(order.shape[0])[None, :], deal[0][None, :], 0), axis=1
    )
    spots = jnp.arange(order.shape[0], dtype=jnp.int32)
    where_is = jnp.sum(
        jnp.where(blocks[None, :] == spots[:, None], spots[None, :], 0), axis=1
    ).astype(jnp.int32)
    info = jnp.concatenate([where_is, lengths])
    info, blocks = after((info, blocks), dealt)
    positions = (blocks[:, None] * BLK + jnp.arange(BLK, dtype=jnp.int32)[None, :]).reshape(-1)
    frequency = THETA ** (-(jnp.arange(head_size // 2, dtype=jnp.float32) * 2.0 / head_size))
    angles = wide(positions)[:, None] * frequency[None, :]
    cosine, sine = jnp.cos(angles), jnp.sin(angles)
    cosine = jnp.concatenate([cosine, cosine], axis=1)
    sine = jnp.concatenate([-sine, sine], axis=1)
    query_scale = wide(query_gain)[None, :]
    key_scale = wide(key_gain)[None, :]

    own = lax.dynamic_slice_in_dim(tokens, core * half_rows, half_rows, 0)
    inputs = wide(own)
    rstd = lax.rsqrt(jnp.mean(inputs * inputs, axis=1, keepdims=True) + EPS)
    normed = gather_rows(after(low(inputs * rstd), dealt), (info, cosine, sine))

    feed_dealt = deal_out(
        [low(wide(after(w, normed[2:6])) * feed_scale) for w in (w_gate, w_up)],
        spot,
        (units, units),
        1,
    )
    feed_weight = gather_stages(in_order(feed_dealt, spot, 0))
    down_dealt = deal_out([after(w_down, feed_dealt).T], spot, (units,), 1)

    valid = positions[:half_rows] < lengths[0]
    seed = lax.dynamic_slice_in_dim(cotangent, core * half_rows, half_rows, 0)
    seed = jnp.where(valid[:, None], seed, 0).astype(jnp.bfloat16)

    seed_own, seed_x, seed_y = gather_near(after(seed, normed[2:]))

    proj, qkv, mixed, mixed_low, recip = attend_forward(
        info, normed, attn_weight, cosine, sine, query_scale, key_scale, heads
    )
    mixed_low, seed_x, seed_y, down_dealt = lax.optimization_barrier(
        (mixed_low, seed_x, seed_y, down_dealt)
    )
    down_weight = gather_stages(in_order(down_dealt, spot, 0))
    seed_rest = gather_far(seed_x, seed_y)
    parts, _ = scatter_rows(
        [mixed_low], attn_weight, proj_cols // query_cols, (seed_own, seed_rest)
    )
    sums, _ = scatter_end(parts)
    seed_far = [other_core(v) for v in after(seed_rest[2:], parts[0])]
    seeds = [seed, seed_own, seed_x, seed_rest[0], seed_y, *seed_rest[1:]] + seed_far
    sums = after(sums, seed_far)
    hidden, hat_two = settle("norm", sums, (own,), (jnp.float32, jnp.bfloat16))

    other, by_x, by_y = gather_near(hat_two)
    filled = feed_expand([[hat_two, other]], 0, feed_weight, local_rows * CTX)
    by_x, by_y = after((by_x, by_y), filled[0])
    x_other, y_other, far_top, far_bottom = gather_far(by_x, by_y)
    filled = feed_expand([[by_x, x_other], [by_y, y_other]], 1, feed_weight, local_rows * CTX, filled)
    far = list(after((far_top, far_bottom), filled[0]))
    far += [other_core(v) for v in far]
    slope, silu, inner = feed_expand([far], 3, feed_weight, local_rows * CTX, filled)
    normed_two = [hat_two, other, by_x, x_other, by_y, y_other] + far
    grad_down = weight_terms([(seeds, [inner])])
    down_weight, grad_down = lax.optimization_barrier((down_weight, grad_down))
    grad_down = sum_stages(grad_down)
    dgate, dup = feed_back(seeds, down_weight, slope, silu)
    parts, _ = scatter_rows([dgate, dup], feed_weight, 0)
    sums, sent = scatter_end(parts)
    grad_feed = weight_terms([(normed_two, [after(dgate, sent), dup])])
    sums, grad_feed = lax.optimization_barrier((sums, grad_feed))
    grad_feed = sum_stages(after(grad_feed, grad_down))
    grad_hidden, grad_attn = settle("back", sums, (hidden, seed), (jnp.float32, jnp.bfloat16))

    feed_parts, _ = scatter_rows([after(inner, grad_attn)], down_weight, 0)
    grad_attn = gather_rows(grad_attn)
    grad_attn = after(grad_attn, feed_parts[0], feed_parts[5])
    grad_proj, gain_sums = attend_backward(
        info, grad_attn, attn_weight, proj, qkv, mixed, recip, cosine, sine, query_scale, key_scale, heads
    )
    down_pieces = dealt_rows(grad_down)
    grad_proj, down_pieces, feed_parts = lax.optimization_barrier(
        (grad_proj, down_pieces, feed_parts)
    )
    grad_attn_w = weight_terms([(normed, [grad_proj]), (grad_attn, [mixed_low])])
    parts, far = scatter_rows([grad_proj], after(attn_weight, grad_attn_w), 0)
    feed_sums, _ = scatter_end(feed_parts, far)
    sums, sent = scatter_end(parts, feed_sums[0])
    grad_attn_w = sum_stages(after(grad_attn_w, grad_feed))
    (grad_tokens_half,) = settle("back", sums, (own, grad_hidden), (jnp.float32,))
    (output_half,) = settle("add", after(feed_sums, grad_tokens_half), (hidden,), (jnp.bfloat16,))

    def whole_rows(values):
        other = other_core(values)
        first = core == 0
        return jnp.concatenate(
            [jnp.where(first, values, other), jnp.where(first, other, values)], axis=0
        )

    def cut(pieces, start, size):
        return wide(in_order([p[:, start : start + size] for p in pieces], spot, 1))

    grad_down_w = cut(down_pieces, 0, units).T
    feed_pieces = dealt_rows(after(grad_feed, sent))
    grad_gate_w = cut(feed_pieces, 0, units)
    grad_up_w = cut(feed_pieces, units, units)
    proj_pieces = dealt_rows(after(grad_attn_w, grad_gate_w, grad_up_w))
    grad_query_w = cut(proj_pieces, 0, query_cols)
    grad_key_w = cut(proj_pieces, query_cols, head_size)
    grad_value_w = cut(proj_pieces, query_cols + head_size, head_size)
    grad_out_w = cut(proj_pieces, proj_cols, query_cols).T

    def gain_part(pairs):
        return sum(jnp.sum(wide(w) * g, axis=1) for w, g in pairs)

    feed_gain = gain_part(((w_gate, grad_gate_w), (w_up, grad_up_w)))
    norm_gain = gain_part(((w_query, grad_query_w), (w_key, grad_key_w), (w_value, grad_value_w)))
    feed_gain = feed_gain + other_core(feed_gain)
    norm_gain = norm_gain + other_core(norm_gain)
    gain_sums = after(gain_sums, grad_tokens_half)
    gain_sums = gain_sums + other_core(gain_sums)
    for bit in (1, 2):
        gain_sums = gain_sums + across(gain_sums, bit)
    gain_sums = lax.psum(gain_sums, "fsdp")
    return (
        whole_rows(output_half),
        whole_rows(grad_tokens_half),
        norm_gain,
        grad_query_w * attn_scale,
        grad_key_w * attn_scale,
        grad_value_w * attn_scale,
        grad_out_w,
        gain_sums[0],
        gain_sums[1],
        feed_gain,
        grad_gate_w * feed_scale,
        grad_up_w * feed_scale,
        grad_down_w,
    )


def solution(mesh):
    return jax.shard_map(
        on_device,
        mesh=mesh,
        in_specs=(
            P(("fsdp", "ctx"), None),
            P(("fsdp", "ctx"), None),
            P("fsdp"),
            P("fsdp", None),
            P(("fsdp", "ctx")),
            P(("fsdp", "ctx"), "tp"),
            P(("fsdp", "ctx"), "tp"),
            P(("fsdp", "ctx"), "tp"),
            P("tp", ("fsdp", "ctx")),
            P(),
            P(),
            P(("fsdp", "ctx")),
            P(("fsdp", "ctx"), "tp"),
            P(("fsdp", "ctx"), "tp"),
            P("tp", ("fsdp", "ctx")),
        ),
        out_specs=(
            P(("fsdp", "ctx"), None),
            P(("fsdp", "ctx"), None),
            P(("fsdp", "ctx")),
            P(("fsdp", "ctx"), "tp"),
            P(("fsdp", "ctx"), "tp"),
            P(("fsdp", "ctx"), "tp"),
            P("tp", ("fsdp", "ctx")),
            P(),
            P(),
            P(("fsdp", "ctx")),
            P(("fsdp", "ctx"), "tp"),
            P(("fsdp", "ctx"), "tp"),
            P("tp", ("fsdp", "ctx")),
        ),
        check_vma=False,
    )
```

```python
import functools
import math

import jax
import jax.numpy as jnp
from jax import lax
from jax.experimental import pallas as pl
from jax.experimental.pallas import tpu as pltpu
from jax.sharding import PartitionSpec as P

BLK = 128
EPS = 1e-06
THETA = 1000000.0
CTX = 4
LIMIT = 56 * 2**20
TILE = 512
CHUNK = 512


def _dot(a, b, dims):
    return lax.dot_general(a, b, (dims, ((), ())), preferred_element_type=jnp.float32)


def _starts(pieces):
    at, starts = 0, []
    for piece in pieces:
        starts.append(at)
        at += piece.shape[0]
    return starts


def _whole(count):
    return [pl.BlockSpec(memory_space=pltpu.VMEM)] * count


def _fetch(pairs, sem):
    copies = [pltpu.make_async_copy(source, target, sem.at[i]) for i, (source, target) in enumerate(pairs)]
    for copy in copies:
        copy.start()
    return copies


def _forward_kernel(heads, scale, count, info, *refs):
    pieces, refs = refs[:count], refs[count:]
    weight_hbm, cos_hbm, sin_hbm, qg_ref, kg_ref, proj_hbm, low_hbm, mlow_ref, rtot_ref = refs[:9]
    x_s, weight_s, cos_ref, sin_ref, proj_ref, low_ref, q_s, k_s, v_s, sem, out_sem = refs[9:]
    hd = cos_ref.shape[1]
    rows = cos_ref.shape[0]
    cols = proj_ref.shape[1]
    factor = scale * math.log2(math.e)
    starts = _starts(pieces)

    copies = _fetch(
        [(weight_hbm, weight_s)]
        + [(p, x_s.at[pl.ds(at, p.shape[0])]) for p, at in zip(pieces, starts)]
        + [(cos_hbm, cos_ref), (sin_hbm, sin_ref)],
        sem,
    )
    copies[0].wait()
    done = 0
    for i, (piece, start) in enumerate(zip(pieces, starts)):
        copies[i + 1].wait()
        end = start + piece.shape[0]
        if end - done >= CHUNK:
            proj_ref[done:end, :] = _dot(x_s[done:end, :], weight_s[:, :cols], ((1,), (0,)))
            done = end
    copies[-2].wait()
    copies[-1].wait()
    proj_out = pltpu.make_async_copy(proj_ref, proj_hbm, out_sem.at[0])
    proj_out.start()

    @pl.loop(0, rows // BLK)
    def _(block):
        here = pl.ds(pl.multiple_of(block * BLK, BLK), BLK)
        cosine = cos_ref[here, :]
        sine = sin_ref[here, :]
        for h in range(heads + 1):
            u = proj_ref[here, h * hd : (h + 1) * hd]
            gain = qg_ref[...] if h < heads else kg_ref[...]
            n = u * lax.rsqrt(jnp.mean(u * u, axis=1, keepdims=True) + EPS) * gain
            o = (n * cosine + pltpu.roll(n, hd // 2, 1) * sine).astype(jnp.bfloat16)
            low_ref[here, h * hd : (h + 1) * hd] = o
            if h < heads:
                q_s[h, here, :] = o
            else:
                k_s[here, :] = o
        val = proj_ref[here, (heads + 1) * hd :].astype(jnp.bfloat16)
        low_ref[here, (heads + 1) * hd :] = val
        v_s[here, :] = val

    low_out = pltpu.make_async_copy(low_ref, low_hbm, out_sem.at[1])
    low_out.start()
    length = info[rows // BLK]
    per = TILE // BLK

    def gather(ref, tile, *lead):
        parts = [
            ref[lead + (pl.ds(pl.multiple_of(info[tile * per + b] * BLK, BLK), BLK), slice(None))]
            for b in range(per)
        ]
        return jnp.concatenate(parts, axis=0)

    @pl.loop(0, rows // TILE)
    def _(i):
        query = jnp.concatenate([gather(q_s, i, h) for h in range(heads)], axis=0)
        full = jnp.minimum(i, length // TILE)

        def scores(j):
            return jnp.exp2(_dot(query, gather(k_s, j), ((1,), (1,))) * factor)

        def take(expo, j, acc, tot):
            part = expo[:, :hd]
            for b in range(1, TILE // hd):
                part = part + expo[:, b * hd : (b + 1) * hd]
            acc = acc + _dot(expo.astype(jnp.bfloat16), gather(v_s, j), ((1,), (0,)))
            return acc, tot + part

        def step(j, carry):
            return take(scores(j), j, *carry)

        zero = jnp.zeros((heads * TILE, hd), jnp.float32)
        acc, tot = lax.fori_loop(0, full, step, (zero, zero))
        expo = scores(full)
        qpos = i * TILE + lax.rem(lax.broadcasted_iota(jnp.int32, expo.shape, 0), TILE)
        kpos = full * TILE + lax.broadcasted_iota(jnp.int32, expo.shape, 1)
        expo = jnp.where((kpos <= qpos) & (kpos < length), expo, 0.0)
        acc, tot = take(expo, full, acc, tot)
        recip = 1.0 / jnp.sum(tot, axis=1, keepdims=True)
        mixed = acc * recip
        recip = jnp.broadcast_to(recip, mixed.shape)
        for h in range(heads):
            for b in range(per):
                at = pl.ds(pl.multiple_of(info[i * per + b] * BLK, BLK), BLK)
                cut = slice(h * TILE + b * BLK, h * TILE + (b + 1) * BLK)
                lanes = slice(h * hd, (h + 1) * hd)
                mlow_ref[at, lanes] = mixed[cut].astype(jnp.bfloat16)
                rtot_ref[at, lanes] = recip[cut]

    proj_out.wait()
    low_out.wait()


def attend_forward(info, pieces, weight, cosine, sine, query_gain, key_gain, heads):
    rows, hd = cosine.shape
    cols = (heads + 2) * hd
    width = heads * hd
    pairs = rows * rows // 2 * heads
    anywhere = pl.BlockSpec(memory_space=pl.ANY)
    return pl.pallas_call(
        functools.partial(_forward_kernel, heads, hd**-0.5, len(pieces)),
        out_shape=(
            jax.ShapeDtypeStruct((rows, cols), jnp.float32),
            jax.ShapeDtypeStruct((rows, cols), jnp.bfloat16),
            jax.ShapeDtypeStruct((rows, width), jnp.bfloat16),
            jax.ShapeDtypeStruct((rows, width), jnp.float32),
        ),
        in_specs=[pl.BlockSpec(memory_space=pltpu.SMEM)] + [anywhere] * (len(pieces) + 3) + _whole(2),
        out_specs=[anywhere] * 2 + _whole(2),
        scratch_shapes=[
            pltpu.VMEM((rows, weight.shape[0]), jnp.bfloat16),
            pltpu.VMEM(weight.shape, jnp.bfloat16),
            pltpu.VMEM((rows, hd), jnp.float32),
            pltpu.VMEM((rows, hd), jnp.float32),
            pltpu.VMEM((rows, cols), jnp.float32),
            pltpu.VMEM((rows, cols), jnp.bfloat16),
            pltpu.VMEM((heads, rows, hd), jnp.bfloat16),
            pltpu.VMEM((rows, hd), jnp.bfloat16),
            pltpu.VMEM((rows, hd), jnp.bfloat16),
            pltpu.SemaphoreType.DMA((len(pieces) + 3,)),
            pltpu.SemaphoreType.DMA((2,)),
        ],
        compiler_params=pltpu.CompilerParams(vmem_limit_bytes=LIMIT),
        cost_estimate=pl.CostEstimate(
            flops=pairs * hd * 4 + 2 * rows * cols * weight.shape[0],
            bytes_accessed=rows * hd * 100,
            transcendentals=pairs,
        ),
        name="attend_forward",
    )(info, *pieces, weight, cosine, sine, query_gain, key_gain)


def _backward_kernel(heads, scale, count, info, *refs):
    pieces, refs = refs[:count], refs[count:]
    inputs, qg_ref, kg_ref, out_ref, gain_ref = refs[:7], refs[7], refs[8], refs[9], refs[10]
    x_s, weight_ref, low_ref, mixed_ref, rtot_ref, proj_ref, cos_ref, sin_ref = refs[11:19]
    gacc_s, dq_s, dk_s, dv_s, sem = refs[19:]
    hd = cos_ref.shape[1]
    rows = cos_ref.shape[0]
    factor = scale * math.log2(math.e)
    length = info[rows // BLK]
    per = TILE // BLK
    starts = _starts(pieces)

    targets = (weight_ref, low_ref, mixed_ref, rtot_ref, proj_ref, cos_ref, sin_ref)
    loads = list(zip(inputs, targets))
    copies = _fetch(
        loads[:1]
        + [(p, x_s.at[pl.ds(at, p.shape[0])]) for p, at in zip(pieces, starts)]
        + [loads[i] for i in (2, 3, 1, 4, 5, 6)],
        sem,
    )
    dk_s[...] = jnp.zeros_like(dk_s)
    dv_s[...] = jnp.zeros_like(dv_s)
    gain_ref[...] = jnp.zeros_like(gain_ref)
    copies[0].wait()
    done = 0
    for i, (piece, start) in enumerate(zip(pieces, starts)):
        copies[i + 1].wait()
        end = start + piece.shape[0]
        if end - done >= CHUNK:
            grad = _dot(x_s[done:end, :], weight_ref[:, (heads + 2) * hd :], ((1,), (0,)))
            for h in range(heads):
                dq_s[h, done:end, :] = grad[:, h * hd : (h + 1) * hd]
            done = end
    copies[count + 1].wait()
    copies[count + 2].wait()

    @pl.loop(0, rows // BLK)
    def _(block):
        at = pl.ds(pl.multiple_of(block * BLK, BLK), BLK)
        for h in range(heads):
            lanes = slice(h * hd, (h + 1) * hd)
            g = dq_s[h, at, :] * rtot_ref[at, lanes]
            gacc_s[h, at, :] = g.astype(jnp.bfloat16)
            dq_s[h, at, :] = g * mixed_ref[at, lanes].astype(jnp.float32)

    copies[count + 3].wait()

    def spots(tile):
        return [pl.ds(pl.multiple_of(info[tile * per + b] * BLK, BLK), BLK) for b in range(per)]

    @pl.loop(0, pl.cdiv(length, TILE))
    def _(i):
        at = spots(i)
        query = jnp.concatenate(
            [low_ref[s, h * hd : (h + 1) * hd] for h in range(heads) for s in at], axis=0
        )
        gacc = jnp.concatenate([gacc_s[h, s, :] for h in range(heads) for s in at], axis=0)
        terms = jnp.concatenate([dq_s[h, s, :] for h in range(heads) for s in at], axis=0)
        shift = jnp.sum(terms.T, axis=0, keepdims=True)

        def tile(j, dq, masked):
            spot = spots(j)
            key = jnp.concatenate([low_ref[s, heads * hd : (heads + 1) * hd] for s in spot], axis=0)
            val = jnp.concatenate([low_ref[s, (heads + 1) * hd :] for s in spot], axis=0)
            expo = jnp.exp2(_dot(key, query, ((1,), (1,))) * factor)
            if masked:
                kpos = j * TILE + lax.broadcasted_iota(jnp.int32, expo.shape, 0)
                qpos = i * TILE + lax.rem(lax.broadcasted_iota(jnp.int32, expo.shape, 1), TILE)
                expo = jnp.where((kpos <= qpos) & (kpos < length), expo, 0.0)
            probs = _dot(val, gacc, ((1,), (1,)))
            ds = (expo * (probs - shift)).astype(jnp.bfloat16)
            dv = _dot(expo.astype(jnp.bfloat16), gacc, ((1,), (0,)))
            dk = _dot(ds, query, ((1,), (0,)))
            for b, s in enumerate(spot):
                dv_s[s, :] += dv[b * BLK : (b + 1) * BLK]
                dk_s[s, :] += dk[b * BLK : (b + 1) * BLK]
            return dq + _dot(ds, key, ((0,), (0,)))

        zero = jnp.zeros((heads * TILE, hd), jnp.float32)
        dq = lax.fori_loop(0, i, lambda j, dq: tile(j, dq, False), zero)
        dq = tile(i, dq, True) * scale
        for h in range(heads):
            for b, s in enumerate(at):
                dq_s[h, s, :] = dq[h * TILE + b * BLK : h * TILE + (b + 1) * BLK]

    def finish(block):
        at = pl.ds(pl.multiple_of(block * BLK, BLK), BLK)
        cosine = cos_ref[at, :]
        sine = sin_ref[at, :]
        for h in range(heads + 1):
            lanes = slice(h * hd, (h + 1) * hd)
            u = proj_ref[at, lanes]
            r = lax.rsqrt(jnp.mean(u * u, axis=1, keepdims=True) + EPS)
            d = dq_s[h, at, :] if h < heads else dk_s[at, :] * scale
            dn = d * cosine - pltpu.roll(d, hd // 2, 1) * sine
            gain = qg_ref[...] if h < heads else kg_ref[...]
            hat = u * r
            row = 0 if h < heads else 1
            gain_ref[row : row + 1, :] += jnp.sum(dn * hat, axis=0, keepdims=True)
            dg = dn * gain
            du = r * (dg - hat * jnp.mean(dg * hat, axis=1, keepdims=True))
            out_ref[at, lanes] = du.astype(jnp.bfloat16)
        out_ref[at, (heads + 1) * hd :] = dv_s[at, :].astype(jnp.bfloat16)

    for b in range(rows // BLK):

        @pl.when(b * BLK >= pl.cdiv(length, TILE) * TILE)
        def _(b=b):
            at = pl.ds(pl.multiple_of(info[b] * BLK, BLK), BLK)
            for h in range(heads):
                dq_s[h, at, :] = jnp.zeros((BLK, hd), jnp.float32)

    for copy in copies[count + 4 :]:
        copy.wait()

    @pl.loop(0, rows // BLK)
    def _(block):
        finish(block)


def attend_backward(
    info, pieces, weight, proj, low, mixed, rtot, cosine, sine, query_gain, key_gain, heads
):
    rows, hd = cosine.shape
    pairs = rows * rows // 2 * heads
    anywhere = pl.BlockSpec(memory_space=pl.ANY)
    inputs = (weight, low, mixed, rtot, proj, cosine, sine)
    return pl.pallas_call(
        functools.partial(_backward_kernel, heads, hd**-0.5, len(pieces)),
        out_shape=(
            jax.ShapeDtypeStruct((rows, (heads + 2) * hd), jnp.bfloat16),
            jax.ShapeDtypeStruct((8, hd), jnp.float32),
        ),
        in_specs=[pl.BlockSpec(memory_space=pltpu.SMEM)] + [anywhere] * (len(pieces) + 7) + _whole(2),
        out_specs=_whole(2),
        scratch_shapes=[pltpu.VMEM((rows, weight.shape[0]), jnp.bfloat16)]
        + [pltpu.VMEM(v.shape, v.dtype) for v in inputs]
        + [
            pltpu.VMEM((heads, rows, hd), jnp.bfloat16),
            pltpu.VMEM((heads, rows, hd), jnp.float32),
            pltpu.VMEM((rows, hd), jnp.float32),
            pltpu.VMEM((rows, hd), jnp.float32),
            pltpu.SemaphoreType.DMA((len(pieces) + 7,)),
        ],
        compiler_params=pltpu.CompilerParams(vmem_limit_bytes=LIMIT),
        cost_estimate=pl.CostEstimate(
            flops=pairs * hd * 10 + 2 * rows * heads * hd * weight.shape[0],
            bytes_accessed=rows * hd * 140,
            transcendentals=pairs,
        ),
        name="attend_backward",
    )(info, *pieces, *inputs, query_gain, key_gain)


def _expand_kernel(counts, *refs):
    groups = []
    for count in counts:
        groups.append(refs[:count])
        refs = refs[count:]
    gate_w, up_w = refs[:2]
    slope_ref, silu_ref, inner_ref = refs[-3:]
    for row, pieces in enumerate(groups):

        @pl.when(pl.program_id(0) == row)
        def _(pieces=pieces):
            for piece, start in zip(pieces, _starts(pieces)):
                at = slice(start, start + piece.shape[0])
                gate = _dot(piece[...], gate_w[...], ((1,), (0,)))
                upper = _dot(piece[...], up_w[...], ((1,), (0,)))
                sigma = 1.0 / (1.0 + jnp.exp(-gate))
                silu = gate * sigma
                slope_ref[at, :] = (upper * sigma * (1.0 + gate - silu)).astype(jnp.bfloat16)
                silu_ref[at, :] = silu.astype(jnp.bfloat16)
                inner_ref[at, :] = (silu * upper).astype(jnp.bfloat16)


def feed_expand(groups, first, weight, rows, filled=(), step=256):
    size = sum(p.shape[0] for p in groups[0])
    width, units = weight.shape[0], weight.shape[1] // 2
    steps = units // step
    pieces = [p for group in groups for p in group]
    tile = pl.BlockSpec((size, step), lambda r, n: (r + first, n))
    done = size * len(groups)
    return pl.pallas_call(
        functools.partial(_expand_kernel, [len(group) for group in groups]),
        grid=(len(groups), steps),
        out_shape=(
            jax.ShapeDtypeStruct((rows, units), jnp.bfloat16),
            jax.ShapeDtypeStruct((rows, units), jnp.bfloat16),
            jax.ShapeDtypeStruct((rows, units), jnp.bfloat16),
        ),
        in_specs=[
            pl.BlockSpec(p.shape, lambda r, n: (0, 0), pipeline_mode=pl.Buffered(1)) for p in pieces
        ]
        + [
            pl.BlockSpec((width, step), lambda r, n: (0, n)),
            pl.BlockSpec((width, step), lambda r, n: (0, n + steps)),
        ]
        + [pl.BlockSpec(memory_space=pl.ANY)] * len(filled),
        out_specs=(tile, tile, tile),
        input_output_aliases={len(pieces) + 2 + i: i for i in range(len(filled))},
        compiler_params=pltpu.CompilerParams(vmem_limit_bytes=LIMIT),
        cost_estimate=pl.CostEstimate(
            flops=4 * done * width * units,
            bytes_accessed=done * width * 2 + width * units * 4 + done * units * 10,
            transcendentals=done * units,
        ),
        name="feed_expand",
    )(*pieces, weight, weight, *filled)


def _shrink_kernel(count, *refs):
    pieces = refs[:count]
    weight, slope_ref, silu_ref, dgate_ref, dup_ref = refs[count:]
    for piece, start in zip(pieces, _starts(pieces)):
        at = slice(start, start + piece.shape[0])
        grad = _dot(piece[...], weight[...], ((1,), (0,)))
        dgate_ref[at, :] = (grad * slope_ref[at, :].astype(jnp.float32)).astype(jnp.bfloat16)
        dup_ref[at, :] = (grad * silu_ref[at, :].astype(jnp.float32)).astype(jnp.bfloat16)


def feed_back(pieces, weight, slope, silu, step=256):
    rows = sum(p.shape[0] for p in pieces)
    width, units = weight.shape
    tile = pl.BlockSpec((rows, step), lambda n: (0, n))
    return pl.pallas_call(
        functools.partial(_shrink_kernel, len(pieces)),
        grid=(units // step,),
        out_shape=(jax.ShapeDtypeStruct((rows, units), jnp.bfloat16),) * 2,
        in_specs=[pl.BlockSpec(p.shape, lambda n: (0, 0), pipeline_mode=pl.Buffered(1)) for p in pieces]
        + [pl.BlockSpec((width, step), lambda n: (0, n)), tile, tile],
        out_specs=(tile, tile),
        compiler_params=pltpu.CompilerParams(vmem_limit_bytes=LIMIT),
        cost_estimate=pl.CostEstimate(
            flops=2 * rows * width * units,
            bytes_accessed=rows * width * 2 + width * units * 2 + rows * units * 12,
            transcendentals=0,
        ),
        name="feed_back",
    )(*pieces, weight, slope, silu)


def _terms_kernel(groups, *refs):
    out_ref, hold_s = refs[-2:]
    refs = refs[:-2]
    column = 0
    for count, sides in groups:
        pieces, others, refs = refs[:count], refs[count : count + sides], refs[count + sides :]
        for piece, start in zip(pieces, _starts(pieces)):
            hold_s[start : start + piece.shape[0], :] = piece[...]
        for other in others:
            size = other.shape[1]
            out_ref[:, column : column + size] = _dot(
                hold_s[...], other[...], ((0,), (0,))
            ).astype(jnp.bfloat16)
            column += size


def weight_terms(groups, step=256):
    width = groups[0][0][0].shape[1]
    rows = groups[0][1][0].shape[0]
    specs, values = [], []
    for pieces, others in groups:
        specs += [pl.BlockSpec((p.shape[0], step), lambda n: (0, n)) for p in pieces]
        specs += [pl.BlockSpec(o.shape, lambda n: (0, 0), pipeline_mode=pl.Buffered(1)) for o in others]
        values += list(pieces) + list(others)
    total = sum(o.shape[1] for _, others in groups for o in others)
    return pl.pallas_call(
        functools.partial(_terms_kernel, [(len(p), len(o)) for p, o in groups]),
        grid=(width // step,),
        out_shape=jax.ShapeDtypeStruct((width, total), jnp.bfloat16),
        in_specs=specs,
        out_specs=pl.BlockSpec((step, total), lambda n: (n, 0)),
        scratch_shapes=[pltpu.VMEM((rows, step), jnp.bfloat16)],
        compiler_params=pltpu.CompilerParams(vmem_limit_bytes=LIMIT),
        cost_estimate=pl.CostEstimate(
            flops=2 * rows * width * total,
            bytes_accessed=sum(v.size * 2 for v in values) + width * total * 2,
            transcendentals=0,
        ),
        name="weight_terms",
    )(*values)


def _rows_kernel(sides, blocks, arrived, cuts, *refs):
    lefts, refs = refs[: sides * blocks], refs[sides * blocks :]
    weight, refs = refs[0], refs[1:]
    there, outs = (refs[0], refs[1:]) if arrived else (None, refs)
    size = lefts[0].shape[0]
    at = 0
    for block in range(blocks):
        column, total = 0, None
        for side in range(sides):
            left = lefts[side * blocks + block]
            depth = left.shape[1]
            term = _dot(left[...], weight[:, column : column + depth], ((1,), (1,)))
            total = term if total is None else total + term
            column += depth
        if arrived:
            total = total + there[block * size : (block + 1) * size, :].astype(jnp.float32)
        row = 0
        while row < size:
            out = outs[cuts[at][0]]
            first, length = cuts[at][1], cuts[at][2]
            out[first : first + length, :] = total[row : row + length].astype(out.dtype)
            row += length
            at += 1


def rows_product(lefts, weight, column, picks, outs, cuts, there=None, size=256, step=512):
    width = weight.shape[0]
    depth = sum(v.shape[1] for v in lefts)
    specs = [
        pl.BlockSpec((size, v.shape[1]), lambda n, p=p: (p, 0), pipeline_mode=pl.Buffered(1))
        for v in lefts
        for p in picks
    ]
    specs.append(pl.BlockSpec((step, depth), lambda n: (n, column)))
    values = [v for v in lefts for _ in picks] + [weight]
    if there is not None:
        specs.append(pl.BlockSpec((there.shape[0], step), lambda n: (0, n)))
        values.append(there)
    rows = size * len(picks)
    return pl.pallas_call(
        functools.partial(_rows_kernel, len(lefts), len(picks), there is not None, cuts),
        grid=(width // step,),
        out_shape=[jax.ShapeDtypeStruct((r, width), t) for r, t in outs],
        in_specs=specs,
        out_specs=[pl.BlockSpec((r, step), lambda n: (0, n)) for r, _ in outs],
        compiler_params=pltpu.CompilerParams(vmem_limit_bytes=LIMIT),
        cost_estimate=pl.CostEstimate(
            flops=2 * rows * width * depth,
            bytes_accessed=rows * depth * 2 + width * depth * 2 + rows * width * 6,
            transcendentals=0,
        ),
        name="rows_product",
    )(*values)


def _settle_kernel(mode, twice, place, *refs):
    total_ref, x_top, x_bottom, y_top, y_bottom = refs[:5]
    rest = refs[5:]
    if twice:
        rest, full_ref = rest[:-1], rest[-1]

    def finish(by_x, by_y):
        step = 16
        for start in range(0, total_ref.shape[0], step):
            here = slice(start, start + step)
            total = total_ref[here, :] + by_x[here, :].astype(jnp.float32) + by_y[here, :].astype(jnp.float32)
            if mode == "add":
                base_ref, out_ref = rest
                out = (base_ref[here, :] + total).astype(out_ref.dtype)
                out_ref[here, :] = out
            elif mode == "norm":
                base_ref, out_ref, hat_ref = rest
                hidden = base_ref[here, :].astype(jnp.float32) + total
                out_ref[here, :] = hidden
                rstd = lax.rsqrt(jnp.mean(hidden * hidden, axis=1, keepdims=True) + EPS)
                hat_ref[here, :] = (hidden * rstd).astype(jnp.bfloat16)
            else:
                source_ref, base_ref = rest[:2]
                source = source_ref[here, :].astype(jnp.float32)
                rstd = lax.rsqrt(jnp.mean(source * source, axis=1, keepdims=True) + EPS)
                hat = source * rstd
                grad = total - hat * jnp.mean(total * hat, axis=1, keepdims=True)
                out = base_ref[here, :].astype(jnp.float32) + rstd * grad
                rest[2][here, :] = out
                if len(rest) > 3:
                    rest[3][here, :] = out.astype(jnp.bfloat16)
            if twice:
                full_ref[here, :] = out

    upper = pl.program_id(0) < pl.num_programs(0) // 2

    @pl.when(upper)
    def _():
        finish(x_top, y_top)

    @pl.when(jnp.logical_not(upper))
    def _():
        finish(x_bottom, y_bottom)


def settle(mode, sums, others, types, core=None, steps=4):
    rows, width = sums[0].shape
    block = (rows // steps, width)
    half = steps // 2
    straight = pl.BlockSpec(block, lambda i, place: (i, 0))
    first = pl.BlockSpec(block, lambda i, place: (jnp.minimum(i, half - 1), 0))
    second = pl.BlockSpec(block, lambda i, place: (jnp.maximum(i - half, 0), 0))
    shapes = [jax.ShapeDtypeStruct((rows, width), t) for t in types]
    out_specs = [straight] * len(types)
    if core is not None:
        shapes.append(jax.ShapeDtypeStruct((2 * rows, width), types[0]))
        out_specs.append(pl.BlockSpec(block, lambda i, place: (place[0] * steps + i, 0)))
    place = jnp.zeros((1,), jnp.int32) if core is None else core.astype(jnp.int32).reshape(1)
    return pl.pallas_call(
        functools.partial(_settle_kernel, mode, core is not None),
        out_shape=shapes,
        grid_spec=pltpu.PrefetchScalarGridSpec(
            num_scalar_prefetch=1,
            grid=(steps,),
            in_specs=[straight, first, second, first, second] + [straight] * len(others),
            out_specs=out_specs,
        ),
        compiler_params=pltpu.CompilerParams(vmem_limit_bytes=LIMIT),
        cost_estimate=pl.CostEstimate(
            flops=rows * width * 10, bytes_accessed=rows * width * 20, transcendentals=rows
        ),
        name="settle",
    )(place, *sums, *others)


def low(values):
    return values.astype(jnp.bfloat16)


def wide(values):
    return values.astype(jnp.float32)


def after(values, *others):
    return lax.optimization_barrier((values,) + others)[0]


def across(values, bits):
    return lax.ppermute(values, "ctx", [(i, i ^ bits) for i in range(CTX)])


def other_core(values):
    return lax.ppermute(values, "tp", [(0, 1), (1, 0)])


def in_order(pieces, spot, axis):
    for bit in (1, 2):
        odd = (spot & bit) != 0
        pieces = [jnp.where(odd, pieces[j ^ bit], pieces[j]) for j in range(CTX)]
    return jnp.concatenate(pieces, axis=axis)


def gather_near(own):
    return other_core(own), across(own, 1), across(own, 2)


def gather_far(by_x, by_y):
    half = by_x.shape[0] // 2
    return other_core(by_x), other_core(by_y), across(by_x[:half], 2), across(by_y[half:], 1)


def gather_rows(own, beside=(), beside_far=()):
    own_other, by_x, by_y = gather_near(own)
    by_x, by_y = after((by_x, by_y), beside)
    x_other, y_other, far_top, far_bottom = gather_far(by_x, by_y)
    far_top, far_bottom = after((far_top, far_bottom), beside_far)
    far = [far_top, far_bottom, other_core(far_top), other_core(far_bottom)]
    return [own, own_other, by_x, x_other, by_y, y_other] + far


def scatter_rows(lefts, weight, column):
    size = lefts[0].shape[0] // (2 * CTX)
    half = size // 2
    wide_step = weight.shape[0] // 2
    far_there = rows_product(
        lefts, weight, column, (7,), [(size, jnp.bfloat16)], [(0, 0, size)], step=wide_step
    )[0]
    rest_there = rows_product(
        lefts,
        after(weight, far_there),
        column,
        (1, 3, 5),
        [(3 * size, jnp.bfloat16)],
        [(0, i * size, size) for i in range(3)],
    )[0]
    far_there = after(other_core(far_there), rest_there)
    rest_there = other_core(rest_there)
    far_top, far_bottom = rows_product(
        lefts,
        weight,
        column,
        (6,),
        [(half, jnp.bfloat16)] * 2,
        [(0, 0, half), (1, 0, half)],
        far_there,
        step=wide_step,
    )
    own, x_top, x_bottom, y_top, y_bottom = rows_product(
        lefts,
        after(weight, far_top),
        column,
        (0, 2, 4),
        [(size, jnp.float32)]
        + [(half, t) for t in (jnp.bfloat16, jnp.float32, jnp.float32, jnp.bfloat16)],
        [(0, 0, size)] + [(i, 0, half) for i in range(1, 5)],
        rest_there,
    )
    return far_top, far_bottom, own, x_top, x_bottom, y_top, y_bottom


def scatter_send(parts):
    far_top, far_bottom, own, x_top, x_bottom, y_top, y_bottom = parts
    to_y = across(far_top, 1)
    to_x = across(far_bottom, 2)
    return own, across(x_top, 1), across(y_bottom, 2), to_x, to_y, x_bottom, y_top


def scatter_end(parts, beside=()):
    own, from_x_top, from_y_bottom, to_x, to_y, x_bottom, y_top = parts
    to_x, to_y = after((to_x, to_y), own, beside)
    x_bottom = low(x_bottom + wide(to_x))
    y_top = low(y_top + wide(to_y))
    return [own, from_x_top, across(x_bottom, 1), across(y_top, 2), from_y_bottom], (x_bottom, y_top)


def deal_out(values, spot, size, axis):
    got = []
    for j in range(CTX):
        piece = [
            lax.dynamic_slice_in_dim(v, (spot ^ j) * n, n, axis) for v, n in zip(values, size)
        ]
        piece = jnp.concatenate(piece, axis=axis) if len(piece) > 1 else piece[0]
        got.append(across(piece, j) if j else piece)
    return got


def gather_stages(shard):
    return lax.all_gather(shard, "fsdp", axis=0, tiled=True)


def sum_stages(values):
    return lax.psum_scatter(values, "fsdp", scatter_dimension=0, tiled=True)


def sum_small(values):
    count = lax.axis_size("fsdp")
    if count & (count - 1):
        return lax.psum(values, "fsdp")
    bit = 1
    while bit < count:
        values = values + lax.ppermute(values, "fsdp", [(i, i ^ bit) for i in range(count)])
        bit *= 2
    return values


def on_device(
    tokens,
    cotangent,
    lengths,
    deal,
    attn_gain,
    w_query,
    w_key,
    w_value,
    w_out,
    query_gain,
    key_gain,
    ffn_gain,
    w_gate,
    w_up,
    w_down,
):
    stages = lax.axis_size("fsdp")
    spot = lax.axis_index("ctx")
    core = lax.axis_index("tp")
    local_rows, width = tokens.shape
    head_size = query_gain.shape[0]
    half_rows = local_rows // 2
    heads = w_query.shape[1] // head_size // CTX
    query_cols = heads * head_size
    proj_cols = query_cols + 2 * head_size
    units = w_gate.shape[1] // CTX
    shard = width // stages // CTX

    def dealt_rows(values):
        got = [
            lax.dynamic_slice_in_dim(values, (spot ^ j) * shard, shard, 0) for j in range(CTX)
        ]
        return [across(v, j) if j else v for j, v in enumerate(got)]

    attn_scale = wide(attn_gain)[:, None]
    feed_scale = wide(ffn_gain)[:, None]
    scaled = [low(wide(w) * attn_scale) for w in (w_query, w_key, w_value)]
    dealt = deal_out(scaled + [w_out.T], spot, (query_cols, head_size, head_size, query_cols), 1)
    attn_weight = gather_stages(in_order(dealt, spot, 0))

    per_half = half_rows // BLK
    order = jnp.arange(deal.shape[1], dtype=jnp.int32).reshape(CTX, 2, per_half)
    chips = jnp.arange(CTX, dtype=jnp.int32) ^ spot
    cores = jnp.arange(2, dtype=jnp.int32) ^ core
    order = ((chips[:, None] * 2 + cores[None, :])[:, :, None] * per_half + order[0, 0]).reshape(-1)
    blocks = jnp.sum(
        jnp.where(order[:, None] == jnp.arange(order.shape[0])[None, :], deal[0][None, :], 0), axis=1
    )
    spots = jnp.arange(order.shape[0], dtype=jnp.int32)
    where_is = jnp.sum(
        jnp.where(blocks[None, :] == spots[:, None], spots[None, :], 0), axis=1
    ).astype(jnp.int32)
    info = jnp.concatenate([where_is, lengths])
    info, blocks = after((info, blocks), dealt)
    positions = (blocks[:, None] * BLK + jnp.arange(BLK, dtype=jnp.int32)[None, :]).reshape(-1)
    frequency = THETA ** (-(jnp.arange(head_size // 2, dtype=jnp.float32) * 2.0 / head_size))
    angles = wide(positions)[:, None] * frequency[None, :]
    cosine, sine = jnp.cos(angles), jnp.sin(angles)
    cosine = jnp.concatenate([cosine, cosine], axis=1)
    sine = jnp.concatenate([-sine, sine], axis=1)
    query_scale = wide(query_gain)[None, :]
    key_scale = wide(key_gain)[None, :]

    own = lax.dynamic_slice_in_dim(tokens, core * half_rows, half_rows, 0)
    inputs = wide(own)
    rstd = lax.rsqrt(jnp.mean(inputs * inputs, axis=1, keepdims=True) + EPS)
    normed_own = after(low(inputs * rstd), dealt)
    other, by_x, by_y = gather_near(normed_own)
    by_x, by_y = after((by_x, by_y), info, cosine, sine)
    feed_scaled = [low(wide(after(w, dealt)) * feed_scale) for w in (w_gate, w_up)]
    down_turned = after(w_down, dealt).T
    by_x, by_y = after((by_x, by_y), feed_scaled, down_turned)
    feed_dealt = deal_out(
        [after(w, by_x) for w in feed_scaled + [down_turned]], spot, (units,) * 3, 1
    )
    x_other, y_other, far_top, far_bottom = gather_far(by_x, by_y)
    far = [far_top, far_bottom, other_core(far_top), other_core(far_bottom)]
    normed = [normed_own, other, by_x, x_other, by_y, y_other] + far
    feed_weight = gather_stages(in_order([v[:, : 2 * units] for v in feed_dealt], spot, 0))
    down_weight = gather_stages(in_order([v[:, 2 * units :] for v in feed_dealt], spot, 0))

    valid = positions[:half_rows] < lengths[0]
    seed = lax.dynamic_slice_in_dim(cotangent, core * half_rows, half_rows, 0)
    seed = jnp.where(valid[:, None], seed, 0).astype(jnp.bfloat16)

    seed_other, seed_x, seed_y = gather_near(after(seed, far_top, far_bottom))
    proj, qkv, mixed_low, recip = attend_forward(
        info, normed, attn_weight, cosine, sine, query_scale, key_scale, heads
    )
    out_column = proj_cols // query_cols
    mixed_low, seed_x, seed_y = lax.optimization_barrier((mixed_low, seed_x, seed_y))
    seed_far = gather_far(seed_x, seed_y)
    parts = list(scatter_rows([mixed_low], attn_weight, out_column))
    parts[0], seed_far = lax.optimization_barrier((parts[0], seed_far))
    parts = scatter_send(parts)
    sums, _ = scatter_end(parts)
    seeds = [seed, seed_other, seed_x, seed_far[0], seed_y, *seed_far[1:]]
    seeds += [other_core(v) for v in seed_far[2:]]
    hidden, hat_two = settle("norm", sums, (own,), (jnp.float32, jnp.bfloat16))

    total = local_rows * CTX
    other, by_x, by_y = gather_near(hat_two)
    x_other, y_other, far_top, far_bottom = gather_far(by_x, by_y)
    filled = feed_expand([[hat_two, other]], 0, feed_weight, total)
    filled = feed_expand([[by_x, x_other], [by_y, y_other]], 1, feed_weight, total, filled)
    far = list(after((far_top, far_bottom), filled[0]))
    far += [other_core(v) for v in far]
    normed_two = [hat_two, other, by_x, x_other, by_y, y_other] + far
    slope, silu, inner = feed_expand([far], 3, feed_weight, total, filled)
    grad_down = weight_terms([(seeds, [inner])])
    down_weight, grad_down = lax.optimization_barrier((down_weight, grad_down))
    grad_down = sum_stages(grad_down)
    dgate, dup = feed_back(seeds, down_weight, slope, silu)
    sums, sent = scatter_end(scatter_send(scatter_rows([dgate, dup], feed_weight, 0)))
    grad_feed = weight_terms([(normed_two, [after(dgate, sent), dup])])
    sums, grad_feed = lax.optimization_barrier((sums, grad_feed))
    grad_feed = sum_stages(after(grad_feed, grad_down))
    grad_hidden, grad_attn = settle("back", sums, (hidden, seed), (jnp.float32, jnp.bfloat16))

    feed_parts = scatter_rows([after(inner, grad_attn)], down_weight, 0)
    grad_attn = gather_rows(grad_attn, feed_parts[:2], feed_parts[2])
    feed_parts = scatter_send(after(feed_parts, grad_attn[6:8]))
    grad_proj, gain_sums = attend_backward(
        info,
        grad_attn,
        attn_weight,
        proj,
        qkv,
        mixed_low,
        recip,
        cosine,
        sine,
        query_scale,
        key_scale,
        heads,
    )
    grad_proj, feed_parts = lax.optimization_barrier((grad_proj, feed_parts))
    down_pieces = dealt_rows(after(grad_down, grad_proj))
    grad_attn_w = weight_terms([(normed, [grad_proj]), (grad_attn, [mixed_low])])
    weight = after(attn_weight, grad_attn_w)
    grad_attn_w = sum_stages(after(grad_attn_w, grad_feed))
    feed_sums, feed_sent = scatter_end(feed_parts, down_pieces)
    feed_pieces = dealt_rows(after(grad_feed, feed_sent))
    parts = list(scatter_rows([grad_proj], after(weight, feed_sent), 0))
    parts[0], feed_pieces = lax.optimization_barrier((parts[0], feed_pieces))
    sums, sent = scatter_end(scatter_send(parts), feed_sums)
    gain_sums = after(gain_sums, sent)
    gain_sums = gain_sums + other_core(gain_sums)
    for bit in (1, 2):
        gain_sums = gain_sums + across(gain_sums, bit)
    gain_sums = sum_small(gain_sums)
    tokens_half, grad_tokens = settle("back", sums, (own, grad_hidden), (jnp.float32,), core)
    feed_sums = after(feed_sums, tokens_half)
    output_half, output = settle("add", feed_sums, (hidden,), (jnp.bfloat16,), core)

    def whole_rows(both, half):
        return lax.dynamic_update_slice_in_dim(both, other_core(half), (1 - core) * half_rows, 0)

    def cut(pieces, start, size):
        return wide(in_order([p[:, start : start + size] for p in pieces], spot, 1))

    grad_down_w = cut(down_pieces, 0, units).T
    grad_gate_w = cut(feed_pieces, 0, units)
    grad_up_w = cut(feed_pieces, units, units)
    output = whole_rows(output, output_half)
    grad_tokens = whole_rows(grad_tokens, tokens_half)
    feed_gain = jnp.sum(wide(w_gate) * grad_gate_w + wide(w_up) * grad_up_w, axis=1)
    feed_gain = feed_gain + other_core(feed_gain)
    proj_pieces = dealt_rows(grad_attn_w)
    grad_query_w = cut(proj_pieces, 0, query_cols)
    grad_key_w = cut(proj_pieces, query_cols, head_size)
    grad_value_w = cut(proj_pieces, query_cols + head_size, head_size)
    grad_out_w = cut(proj_pieces, proj_cols, query_cols).T

    pairs = ((w_query, grad_query_w), (w_key, grad_key_w), (w_value, grad_value_w))
    norm_gain = sum(jnp.sum(wide(w) * g, axis=1) for w, g in pairs)
    norm_gain = norm_gain + other_core(norm_gain)
    return (
        output,
        grad_tokens,
        norm_gain,
        grad_query_w * attn_scale,
        grad_key_w * attn_scale,
        grad_value_w * attn_scale,
        grad_out_w,
        gain_sums[0],
        gain_sums[1],
        feed_gain,
        grad_gate_w * feed_scale,
        grad_up_w * feed_scale,
        grad_down_w,
    )


def solution(mesh):
    return jax.shard_map(
        on_device,
        mesh=mesh,
        in_specs=(
            P(("fsdp", "ctx"), None),
            P(("fsdp", "ctx"), None),
            P("fsdp"),
            P("fsdp", None),
            P(("fsdp", "ctx")),
            P(("fsdp", "ctx"), "tp"),
            P(("fsdp", "ctx"), "tp"),
            P(("fsdp", "ctx"), "tp"),
            P("tp", ("fsdp", "ctx")),
            P(),
            P(),
            P(("fsdp", "ctx")),
            P(("fsdp", "ctx"), "tp"),
            P(("fsdp", "ctx"), "tp"),
            P("tp", ("fsdp", "ctx")),
        ),
        out_specs=(
            P(("fsdp", "ctx"), None),
            P(("fsdp", "ctx"), None),
            P(("fsdp", "ctx")),
            P(("fsdp", "ctx"), "tp"),
            P(("fsdp", "ctx"), "tp"),
            P(("fsdp", "ctx"), "tp"),
            P("tp", ("fsdp", "ctx")),
            P(),
            P(),
            P(("fsdp", "ctx")),
            P(("fsdp", "ctx"), "tp"),
            P(("fsdp", "ctx"), "tp"),
            P("tp", ("fsdp", "ctx")),
        ),
        check_vma=False,
    )
```

```python
import functools
import math

import jax
import jax.numpy as jnp
from jax import lax
from jax.experimental import pallas as pl
from jax.experimental.pallas import tpu as pltpu
from jax.sharding import PartitionSpec as P

BLK = 128
EPS = 1e-06
THETA = 1000000.0
CTX = 4
LIMIT = 56 * 2**20
TILE = 512
CHUNK = 512


def _dot(a, b, dims):
    return lax.dot_general(a, b, (dims, ((), ())), preferred_element_type=jnp.float32)


def _starts(pieces):
    at, starts = 0, []
    for piece in pieces:
        starts.append(at)
        at += piece.shape[0]
    return starts


def _whole(count):
    return [pl.BlockSpec(memory_space=pltpu.VMEM)] * count


def _fetch(pairs, sem):
    copies = [pltpu.make_async_copy(source, target, sem.at[i]) for i, (source, target) in enumerate(pairs)]
    for copy in copies:
        copy.start()
    return copies


def _forward_kernel(heads, scale, count, info, *refs):
    pieces, refs = refs[:count], refs[count:]
    weight_hbm, cos_hbm, sin_hbm, qg_ref, kg_ref, proj_hbm, low_hbm, mlow_ref, rtot_ref = refs[:9]
    x_s, weight_s, cos_ref, sin_ref, proj_ref, low_ref, q_s, k_s, v_s, sem, out_sem = refs[9:]
    hd = cos_ref.shape[1]
    rows = cos_ref.shape[0]
    cols = proj_ref.shape[1]
    factor = scale * math.log2(math.e)
    starts = _starts(pieces)

    copies = _fetch(
        [(weight_hbm, weight_s)]
        + [(p, x_s.at[pl.ds(at, p.shape[0])]) for p, at in zip(pieces, starts)]
        + [(cos_hbm, cos_ref), (sin_hbm, sin_ref)],
        sem,
    )
    copies[0].wait()
    done = 0
    for i, (piece, start) in enumerate(zip(pieces, starts)):
        copies[i + 1].wait()
        end = start + piece.shape[0]
        if end - done >= CHUNK:
            proj_ref[done:end, :] = _dot(x_s[done:end, :], weight_s[:, :cols], ((1,), (0,)))
            done = end
    copies[-2].wait()
    copies[-1].wait()
    proj_out = pltpu.make_async_copy(proj_ref, proj_hbm, out_sem.at[0])
    proj_out.start()

    @pl.loop(0, rows // BLK)
    def _(block):
        here = pl.ds(pl.multiple_of(block * BLK, BLK), BLK)
        cosine = cos_ref[here, :]
        sine = sin_ref[here, :]
        for h in range(heads + 1):
            u = proj_ref[here, h * hd : (h + 1) * hd]
            gain = qg_ref[...] if h < heads else kg_ref[...]
            n = u * lax.rsqrt(jnp.mean(u * u, axis=1, keepdims=True) + EPS) * gain
            o = (n * cosine + pltpu.roll(n, hd // 2, 1) * sine).astype(jnp.bfloat16)
            low_ref[here, h * hd : (h + 1) * hd] = o
            if h < heads:
                q_s[h, here, :] = o
            else:
                k_s[here, :] = o
        val = proj_ref[here, (heads + 1) * hd :].astype(jnp.bfloat16)
        low_ref[here, (heads + 1) * hd :] = val
        v_s[here, :] = val

    low_out = pltpu.make_async_copy(low_ref, low_hbm, out_sem.at[1])
    low_out.start()
    length = info[rows // BLK]
    per = TILE // BLK

    def gather(ref, tile, *lead):
        parts = [
            ref[lead + (pl.ds(pl.multiple_of(info[tile * per + b] * BLK, BLK), BLK), slice(None))]
            for b in range(per)
        ]
        return jnp.concatenate(parts, axis=0)

    @pl.loop(0, rows // TILE)
    def _(i):
        query = jnp.concatenate([gather(q_s, i, h) for h in range(heads)], axis=0)
        full = jnp.minimum(i, length // TILE)

        def scores(j):
            return jnp.exp2(_dot(query, gather(k_s, j), ((1,), (1,))) * factor)

        def take(expo, j, acc, tot):
            part = expo[:, :hd]
            for b in range(1, TILE // hd):
                part = part + expo[:, b * hd : (b + 1) * hd]
            acc = acc + _dot(expo.astype(jnp.bfloat16), gather(v_s, j), ((1,), (0,)))
            return acc, tot + part

        def step(j, carry):
            return take(scores(j), j, *carry)

        zero = jnp.zeros((heads * TILE, hd), jnp.float32)
        acc, tot = lax.fori_loop(0, full, step, (zero, zero))
        expo = scores(full)
        qpos = i * TILE + lax.rem(lax.broadcasted_iota(jnp.int32, expo.shape, 0), TILE)
        kpos = full * TILE + lax.broadcasted_iota(jnp.int32, expo.shape, 1)
        expo = jnp.where((kpos <= qpos) & (kpos < length), expo, 0.0)
        acc, tot = take(expo, full, acc, tot)
        recip = 1.0 / jnp.sum(tot, axis=1, keepdims=True)
        mixed = acc * recip
        recip = jnp.broadcast_to(recip, mixed.shape)
        for h in range(heads):
            for b in range(per):
                at = pl.ds(pl.multiple_of(info[i * per + b] * BLK, BLK), BLK)
                cut = slice(h * TILE + b * BLK, h * TILE + (b + 1) * BLK)
                lanes = slice(h * hd, (h + 1) * hd)
                mlow_ref[at, lanes] = mixed[cut].astype(jnp.bfloat16)
                rtot_ref[at, lanes] = recip[cut]

    proj_out.wait()
    low_out.wait()


def attend_forward(info, pieces, weight, cosine, sine, query_gain, key_gain, heads):
    rows, hd = cosine.shape
    cols = (heads + 2) * hd
    width = heads * hd
    pairs = rows * rows // 2 * heads
    anywhere = pl.BlockSpec(memory_space=pl.ANY)
    return pl.pallas_call(
        functools.partial(_forward_kernel, heads, hd**-0.5, len(pieces)),
        out_shape=(
            jax.ShapeDtypeStruct((rows, cols), jnp.float32),
            jax.ShapeDtypeStruct((rows, cols), jnp.bfloat16),
            jax.ShapeDtypeStruct((rows, width), jnp.bfloat16),
            jax.ShapeDtypeStruct((rows, width), jnp.float32),
        ),
        in_specs=[pl.BlockSpec(memory_space=pltpu.SMEM)] + [anywhere] * (len(pieces) + 3) + _whole(2),
        out_specs=[anywhere] * 2 + _whole(2),
        scratch_shapes=[
            pltpu.VMEM((rows, weight.shape[0]), jnp.bfloat16),
            pltpu.VMEM(weight.shape, jnp.bfloat16),
            pltpu.VMEM((rows, hd), jnp.float32),
            pltpu.VMEM((rows, hd), jnp.float32),
            pltpu.VMEM((rows, cols), jnp.float32),
            pltpu.VMEM((rows, cols), jnp.bfloat16),
            pltpu.VMEM((heads, rows, hd), jnp.bfloat16),
            pltpu.VMEM((rows, hd), jnp.bfloat16),
            pltpu.VMEM((rows, hd), jnp.bfloat16),
            pltpu.SemaphoreType.DMA((len(pieces) + 3,)),
            pltpu.SemaphoreType.DMA((2,)),
        ],
        compiler_params=pltpu.CompilerParams(vmem_limit_bytes=LIMIT),
        cost_estimate=pl.CostEstimate(
            flops=pairs * hd * 4 + 2 * rows * cols * weight.shape[0],
            bytes_accessed=rows * hd * 100,
            transcendentals=pairs,
        ),
        name="attend_forward",
    )(info, *pieces, weight, cosine, sine, query_gain, key_gain)


def _backward_kernel(heads, scale, count, info, *refs):
    pieces, refs = refs[:count], refs[count:]
    inputs, qg_ref, kg_ref, out_ref, gain_ref = refs[:7], refs[7], refs[8], refs[9], refs[10]
    x_s, weight_ref, low_ref, mixed_ref, rtot_ref, proj_ref, cos_ref, sin_ref = refs[11:19]
    gacc_s, dq_s, dk_s, dv_s, sem = refs[19:]
    hd = cos_ref.shape[1]
    rows = cos_ref.shape[0]
    factor = scale * math.log2(math.e)
    length = info[rows // BLK]
    per = TILE // BLK
    starts = _starts(pieces)

    targets = (weight_ref, low_ref, mixed_ref, rtot_ref, proj_ref, cos_ref, sin_ref)
    loads = list(zip(inputs, targets))
    copies = _fetch(
        loads[:1]
        + [(p, x_s.at[pl.ds(at, p.shape[0])]) for p, at in zip(pieces, starts)]
        + [loads[i] for i in (2, 3, 1, 4, 5, 6)],
        sem,
    )
    dk_s[...] = jnp.zeros_like(dk_s)
    dv_s[...] = jnp.zeros_like(dv_s)
    gain_ref[...] = jnp.zeros_like(gain_ref)
    copies[0].wait()
    done = 0
    for i, (piece, start) in enumerate(zip(pieces, starts)):
        copies[i + 1].wait()
        end = start + piece.shape[0]
        if end - done >= CHUNK:
            grad = _dot(x_s[done:end, :], weight_ref[:, (heads + 2) * hd :], ((1,), (0,)))
            for h in range(heads):
                dq_s[h, done:end, :] = grad[:, h * hd : (h + 1) * hd]
            done = end
    copies[count + 1].wait()
    copies[count + 2].wait()

    @pl.loop(0, rows // BLK)
    def _(block):
        at = pl.ds(pl.multiple_of(block * BLK, BLK), BLK)
        for h in range(heads):
            lanes = slice(h * hd, (h + 1) * hd)
            g = dq_s[h, at, :] * rtot_ref[at, lanes]
            gacc_s[h, at, :] = g.astype(jnp.bfloat16)
            dq_s[h, at, :] = g * mixed_ref[at, lanes].astype(jnp.float32)

    copies[count + 3].wait()

    def spots(tile):
        return [pl.ds(pl.multiple_of(info[tile * per + b] * BLK, BLK), BLK) for b in range(per)]

    @pl.loop(0, pl.cdiv(length, TILE))
    def _(i):
        at = spots(i)
        query = jnp.concatenate(
            [low_ref[s, h * hd : (h + 1) * hd] for h in range(heads) for s in at], axis=0
        )
        gacc = jnp.concatenate([gacc_s[h, s, :] for h in range(heads) for s in at], axis=0)
        terms = jnp.concatenate([dq_s[h, s, :] for h in range(heads) for s in at], axis=0)
        shift = jnp.sum(terms.T, axis=0, keepdims=True)

        def tile(j, dq, masked):
            spot = spots(j)
            key = jnp.concatenate([low_ref[s, heads * hd : (heads + 1) * hd] for s in spot], axis=0)
            val = jnp.concatenate([low_ref[s, (heads + 1) * hd :] for s in spot], axis=0)
            expo = jnp.exp2(_dot(key, query, ((1,), (1,))) * factor)
            if masked:
                kpos = j * TILE + lax.broadcasted_iota(jnp.int32, expo.shape, 0)
                qpos = i * TILE + lax.rem(lax.broadcasted_iota(jnp.int32, expo.shape, 1), TILE)
                expo = jnp.where((kpos <= qpos) & (kpos < length), expo, 0.0)
            probs = _dot(val, gacc, ((1,), (1,)))
            ds = (expo * (probs - shift)).astype(jnp.bfloat16)
            dv = _dot(expo.astype(jnp.bfloat16), gacc, ((1,), (0,)))
            dk = _dot(ds, query, ((1,), (0,)))
            for b, s in enumerate(spot):
                dv_s[s, :] += dv[b * BLK : (b + 1) * BLK]
                dk_s[s, :] += dk[b * BLK : (b + 1) * BLK]
            return dq + _dot(ds, key, ((0,), (0,)))

        zero = jnp.zeros((heads * TILE, hd), jnp.float32)
        dq = lax.fori_loop(0, i, lambda j, dq: tile(j, dq, False), zero)
        dq = tile(i, dq, True) * scale
        for h in range(heads):
            for b, s in enumerate(at):
                dq_s[h, s, :] = dq[h * TILE + b * BLK : h * TILE + (b + 1) * BLK]

    def finish(block):
        at = pl.ds(pl.multiple_of(block * BLK, BLK), BLK)
        cosine = cos_ref[at, :]
        sine = sin_ref[at, :]
        for h in range(heads + 1):
            lanes = slice(h * hd, (h + 1) * hd)
            u = proj_ref[at, lanes]
            r = lax.rsqrt(jnp.mean(u * u, axis=1, keepdims=True) + EPS)
            d = dq_s[h, at, :] if h < heads else dk_s[at, :] * scale
            dn = d * cosine - pltpu.roll(d, hd // 2, 1) * sine
            gain = qg_ref[...] if h < heads else kg_ref[...]
            hat = u * r
            row = 0 if h < heads else 1
            gain_ref[row : row + 1, :] += jnp.sum(dn * hat, axis=0, keepdims=True)
            dg = dn * gain
            du = r * (dg - hat * jnp.mean(dg * hat, axis=1, keepdims=True))
            out_ref[at, lanes] = du.astype(jnp.bfloat16)
        out_ref[at, (heads + 1) * hd :] = dv_s[at, :].astype(jnp.bfloat16)

    for b in range(rows // BLK):

        @pl.when(b * BLK >= pl.cdiv(length, TILE) * TILE)
        def _(b=b):
            at = pl.ds(pl.multiple_of(info[b] * BLK, BLK), BLK)
            for h in range(heads):
                dq_s[h, at, :] = jnp.zeros((BLK, hd), jnp.float32)

    for copy in copies[count + 4 :]:
        copy.wait()

    @pl.loop(0, rows // BLK)
    def _(block):
        finish(block)


def attend_backward(
    info, pieces, weight, proj, low, mixed, rtot, cosine, sine, query_gain, key_gain, heads
):
    rows, hd = cosine.shape
    pairs = rows * rows // 2 * heads
    anywhere = pl.BlockSpec(memory_space=pl.ANY)
    inputs = (weight, low, mixed, rtot, proj, cosine, sine)
    return pl.pallas_call(
        functools.partial(_backward_kernel, heads, hd**-0.5, len(pieces)),
        out_shape=(
            jax.ShapeDtypeStruct((rows, (heads + 2) * hd), jnp.bfloat16),
            jax.ShapeDtypeStruct((8, hd), jnp.float32),
        ),
        in_specs=[pl.BlockSpec(memory_space=pltpu.SMEM)] + [anywhere] * (len(pieces) + 7) + _whole(2),
        out_specs=_whole(2),
        scratch_shapes=[pltpu.VMEM((rows, weight.shape[0]), jnp.bfloat16)]
        + [pltpu.VMEM(v.shape, v.dtype) for v in inputs]
        + [
            pltpu.VMEM((heads, rows, hd), jnp.bfloat16),
            pltpu.VMEM((heads, rows, hd), jnp.float32),
            pltpu.VMEM((rows, hd), jnp.float32),
            pltpu.VMEM((rows, hd), jnp.float32),
            pltpu.SemaphoreType.DMA((len(pieces) + 7,)),
        ],
        compiler_params=pltpu.CompilerParams(vmem_limit_bytes=LIMIT),
        cost_estimate=pl.CostEstimate(
            flops=pairs * hd * 10 + 2 * rows * heads * hd * weight.shape[0],
            bytes_accessed=rows * hd * 140,
            transcendentals=pairs,
        ),
        name="attend_backward",
    )(info, *pieces, *inputs, query_gain, key_gain)


def _expand_kernel(counts, *refs):
    groups = []
    for count in counts:
        groups.append(refs[:count])
        refs = refs[count:]
    gate_w, up_w = refs[:2]
    slope_ref, silu_ref, inner_ref = refs[-3:]
    for row, pieces in enumerate(groups):

        @pl.when(pl.program_id(0) == row)
        def _(pieces=pieces):
            for piece, start in zip(pieces, _starts(pieces)):
                at = slice(start, start + piece.shape[0])
                gate = _dot(piece[...], gate_w[...], ((1,), (0,)))
                upper = _dot(piece[...], up_w[...], ((1,), (0,)))
                sigma = 1.0 / (1.0 + jnp.exp(-gate))
                silu = gate * sigma
                slope_ref[at, :] = (upper * sigma * (1.0 + gate - silu)).astype(jnp.bfloat16)
                silu_ref[at, :] = silu.astype(jnp.bfloat16)
                inner_ref[at, :] = (silu * upper).astype(jnp.bfloat16)


def feed_expand(groups, first, weight, rows, filled=(), step=256):
    size = sum(p.shape[0] for p in groups[0])
    width, units = weight.shape[0], weight.shape[1] // 2
    steps = units // step
    pieces = [p for group in groups for p in group]
    tile = pl.BlockSpec((size, step), lambda r, n: (r + first, n))
    done = size * len(groups)
    return pl.pallas_call(
        functools.partial(_expand_kernel, [len(group) for group in groups]),
        grid=(len(groups), steps),
        out_shape=(
            jax.ShapeDtypeStruct((rows, units), jnp.bfloat16),
            jax.ShapeDtypeStruct((rows, units), jnp.bfloat16),
            jax.ShapeDtypeStruct((rows, units), jnp.bfloat16),
        ),
        in_specs=[
            pl.BlockSpec(p.shape, lambda r, n: (0, 0), pipeline_mode=pl.Buffered(1)) for p in pieces
        ]
        + [
            pl.BlockSpec((width, step), lambda r, n: (0, n)),
            pl.BlockSpec((width, step), lambda r, n: (0, n + steps)),
        ]
        + [pl.BlockSpec(memory_space=pl.ANY)] * len(filled),
        out_specs=(tile, tile, tile),
        input_output_aliases={len(pieces) + 2 + i: i for i in range(len(filled))},
        compiler_params=pltpu.CompilerParams(vmem_limit_bytes=LIMIT),
        cost_estimate=pl.CostEstimate(
            flops=4 * done * width * units,
            bytes_accessed=done * width * 2 + width * units * 4 + done * units * 10,
            transcendentals=done * units,
        ),
        name="feed_expand",
    )(*pieces, weight, weight, *filled)


def _shrink_kernel(count, *refs):
    pieces = refs[:count]
    weight, slope_ref, silu_ref, dgate_ref, dup_ref = refs[count:]
    for piece, start in zip(pieces, _starts(pieces)):
        at = slice(start, start + piece.shape[0])
        grad = _dot(piece[...], weight[...], ((1,), (0,)))
        dgate_ref[at, :] = (grad * slope_ref[at, :].astype(jnp.float32)).astype(jnp.bfloat16)
        dup_ref[at, :] = (grad * silu_ref[at, :].astype(jnp.float32)).astype(jnp.bfloat16)


def feed_back(pieces, weight, slope, silu, step=256):
    rows = sum(p.shape[0] for p in pieces)
    width, units = weight.shape
    tile = pl.BlockSpec((rows, step), lambda n: (0, n))
    return pl.pallas_call(
        functools.partial(_shrink_kernel, len(pieces)),
        grid=(units // step,),
        out_shape=(jax.ShapeDtypeStruct((rows, units), jnp.bfloat16),) * 2,
        in_specs=[pl.BlockSpec(p.shape, lambda n: (0, 0), pipeline_mode=pl.Buffered(1)) for p in pieces]
        + [pl.BlockSpec((width, step), lambda n: (0, n)), tile, tile],
        out_specs=(tile, tile),
        compiler_params=pltpu.CompilerParams(vmem_limit_bytes=LIMIT),
        cost_estimate=pl.CostEstimate(
            flops=2 * rows * width * units,
            bytes_accessed=rows * width * 2 + width * units * 2 + rows * units * 12,
            transcendentals=0,
        ),
        name="feed_back",
    )(*pieces, weight, slope, silu)


def _terms_kernel(groups, *refs):
    out_ref, hold_s = refs[-2:]
    refs = refs[:-2]
    column = 0
    for count, sides in groups:
        pieces, others, refs = refs[:count], refs[count : count + sides], refs[count + sides :]
        for piece, start in zip(pieces, _starts(pieces)):
            hold_s[start : start + piece.shape[0], :] = piece[...]
        for other in others:
            size = other.shape[1]
            out_ref[:, column : column + size] = _dot(
                hold_s[...], other[...], ((0,), (0,))
            ).astype(jnp.bfloat16)
            column += size


def weight_terms(groups, step=256):
    width = groups[0][0][0].shape[1]
    rows = groups[0][1][0].shape[0]
    specs, values = [], []
    for pieces, others in groups:
        specs += [pl.BlockSpec((p.shape[0], step), lambda n: (0, n)) for p in pieces]
        specs += [pl.BlockSpec(o.shape, lambda n: (0, 0), pipeline_mode=pl.Buffered(1)) for o in others]
        values += list(pieces) + list(others)
    total = sum(o.shape[1] for _, others in groups for o in others)
    return pl.pallas_call(
        functools.partial(_terms_kernel, [(len(p), len(o)) for p, o in groups]),
        grid=(width // step,),
        out_shape=jax.ShapeDtypeStruct((width, total), jnp.bfloat16),
        in_specs=specs,
        out_specs=pl.BlockSpec((step, total), lambda n: (n, 0)),
        scratch_shapes=[pltpu.VMEM((rows, step), jnp.bfloat16)],
        compiler_params=pltpu.CompilerParams(vmem_limit_bytes=LIMIT),
        cost_estimate=pl.CostEstimate(
            flops=2 * rows * width * total,
            bytes_accessed=sum(v.size * 2 for v in values) + width * total * 2,
            transcendentals=0,
        ),
        name="weight_terms",
    )(*values)


def _rows_kernel(sides, blocks, arrived, cuts, *refs):
    lefts, refs = refs[: sides * blocks], refs[sides * blocks :]
    weight, refs = refs[0], refs[1:]
    there, outs = (refs[0], refs[1:]) if arrived else (None, refs)
    size = lefts[0].shape[0]
    at = 0
    for block in range(blocks):
        column, total = 0, None
        for side in range(sides):
            left = lefts[side * blocks + block]
            depth = left.shape[1]
            term = _dot(left[...], weight[:, column : column + depth], ((1,), (1,)))
            total = term if total is None else total + term
            column += depth
        if arrived:
            total = total + there[block * size : (block + 1) * size, :].astype(jnp.float32)
        row = 0
        while row < size:
            out = outs[cuts[at][0]]
            first, length = cuts[at][1], cuts[at][2]
            out[first : first + length, :] = total[row : row + length].astype(out.dtype)
            row += length
            at += 1


def rows_product(lefts, weight, column, picks, outs, cuts, there=None, size=256, step=512):
    width = weight.shape[0]
    depth = sum(v.shape[1] for v in lefts)
    specs = [
        pl.BlockSpec((size, v.shape[1]), lambda n, p=p: (p, 0), pipeline_mode=pl.Buffered(1))
        for v in lefts
        for p in picks
    ]
    specs.append(pl.BlockSpec((step, depth), lambda n: (n, column)))
    values = [v for v in lefts for _ in picks] + [weight]
    if there is not None:
        specs.append(pl.BlockSpec((there.shape[0], step), lambda n: (0, n)))
        values.append(there)
    rows = size * len(picks)
    return pl.pallas_call(
        functools.partial(_rows_kernel, len(lefts), len(picks), there is not None, cuts),
        grid=(width // step,),
        out_shape=[jax.ShapeDtypeStruct((r, width), t) for r, t in outs],
        in_specs=specs,
        out_specs=[pl.BlockSpec((r, step), lambda n: (0, n)) for r, _ in outs],
        compiler_params=pltpu.CompilerParams(vmem_limit_bytes=LIMIT),
        cost_estimate=pl.CostEstimate(
            flops=2 * rows * width * depth,
            bytes_accessed=rows * depth * 2 + width * depth * 2 + rows * width * 6,
            transcendentals=0,
        ),
        name="rows_product",
    )(*values)


def _settle_kernel(mode, twice, place, *refs):
    total_ref, x_top, x_bottom, y_top, y_bottom = refs[:5]
    rest = refs[5:]
    if twice:
        rest, full_ref = rest[:-1], rest[-1]

    def finish(by_x, by_y):
        step = 16
        for start in range(0, total_ref.shape[0], step):
            here = slice(start, start + step)
            total = total_ref[here, :] + by_x[here, :].astype(jnp.float32) + by_y[here, :].astype(jnp.float32)
            if mode == "add":
                base_ref, out_ref = rest
                out = (base_ref[here, :] + total).astype(out_ref.dtype)
                out_ref[here, :] = out
            elif mode == "norm":
                base_ref, out_ref, hat_ref = rest
                hidden = base_ref[here, :].astype(jnp.float32) + total
                out_ref[here, :] = hidden
                rstd = lax.rsqrt(jnp.mean(hidden * hidden, axis=1, keepdims=True) + EPS)
                hat_ref[here, :] = (hidden * rstd).astype(jnp.bfloat16)
            else:
                source_ref, base_ref = rest[:2]
                source = source_ref[here, :].astype(jnp.float32)
                rstd = lax.rsqrt(jnp.mean(source * source, axis=1, keepdims=True) + EPS)
                hat = source * rstd
                grad = total - hat * jnp.mean(total * hat, axis=1, keepdims=True)
                out = base_ref[here, :].astype(jnp.float32) + rstd * grad
                rest[2][here, :] = out
                if len(rest) > 3:
                    rest[3][here, :] = out.astype(jnp.bfloat16)
            if twice:
                full_ref[here, :] = out

    upper = pl.program_id(0) < pl.num_programs(0) // 2

    @pl.when(upper)
    def _():
        finish(x_top, y_top)

    @pl.when(jnp.logical_not(upper))
    def _():
        finish(x_bottom, y_bottom)


def settle(mode, sums, others, types, core=None, steps=2):
    rows, width = sums[0].shape
    block = (rows // steps, width)
    half = steps // 2
    straight = pl.BlockSpec(block, lambda i, place: (i, 0))
    first = pl.BlockSpec(block, lambda i, place: (jnp.minimum(i, half - 1), 0))
    second = pl.BlockSpec(block, lambda i, place: (jnp.maximum(i - half, 0), 0))
    shapes = [jax.ShapeDtypeStruct((rows, width), t) for t in types]
    out_specs = [straight] * len(types)
    if core is not None:
        shapes.append(jax.ShapeDtypeStruct((2 * rows, width), types[0]))
        out_specs.append(pl.BlockSpec(block, lambda i, place: (place[0] * steps + i, 0)))
    place = jnp.zeros((1,), jnp.int32) if core is None else core.astype(jnp.int32).reshape(1)
    return pl.pallas_call(
        functools.partial(_settle_kernel, mode, core is not None),
        out_shape=shapes,
        grid_spec=pltpu.PrefetchScalarGridSpec(
            num_scalar_prefetch=1,
            grid=(steps,),
            in_specs=[straight, first, second, first, second] + [straight] * len(others),
            out_specs=out_specs,
        ),
        compiler_params=pltpu.CompilerParams(vmem_limit_bytes=LIMIT),
        cost_estimate=pl.CostEstimate(
            flops=rows * width * 10, bytes_accessed=rows * width * 20, transcendentals=rows
        ),
        name="settle",
    )(place, *sums, *others)


def low(values):
    return values.astype(jnp.bfloat16)


def wide(values):
    return values.astype(jnp.float32)


def after(values, *others):
    return lax.optimization_barrier((values,) + others)[0]


def across(values, bits):
    return lax.ppermute(values, "ctx", [(i, i ^ bits) for i in range(CTX)])


def other_core(values):
    return lax.ppermute(values, "tp", [(0, 1), (1, 0)])


def in_order(pieces, spot, axis):
    for bit in (1, 2):
        odd = (spot & bit) != 0
        pieces = [jnp.where(odd, pieces[j ^ bit], pieces[j]) for j in range(CTX)]
    return jnp.concatenate(pieces, axis=axis)


def gather_near(own):
    return other_core(own), across(own, 1), across(own, 2)


def gather_far(by_x, by_y):
    half = by_x.shape[0] // 2
    return other_core(by_x), other_core(by_y), across(by_x[:half], 2), across(by_y[half:], 1)


def gather_rows(own, beside=(), beside_far=()):
    own_other, by_x, by_y = gather_near(own)
    by_x, by_y = after((by_x, by_y), beside)
    x_other, y_other, far_top, far_bottom = gather_far(by_x, by_y)
    far_top, far_bottom = after((far_top, far_bottom), beside_far)
    far = [far_top, far_bottom, other_core(far_top), other_core(far_bottom)]
    return [own, own_other, by_x, x_other, by_y, y_other] + far


def scatter_rows(lefts, weight, column, beside=()):
    size = lefts[0].shape[0] // (2 * CTX)
    half = size // 2
    wide_step = weight.shape[0] // 2
    far_there = rows_product(
        lefts, weight, column, (7,), [(size, jnp.bfloat16)], [(0, 0, size)], step=wide_step
    )[0]
    rest_there = rows_product(
        lefts,
        after(weight, far_there),
        column,
        (1, 3, 5),
        [(3 * size, jnp.bfloat16)],
        [(0, i * size, size) for i in range(3)],
    )[0]
    far_there = after(other_core(far_there), rest_there, beside)
    rest_there = other_core(rest_there)
    far_top, far_bottom = rows_product(
        lefts,
        weight,
        column,
        (6,),
        [(half, jnp.bfloat16)] * 2,
        [(0, 0, half), (1, 0, half)],
        far_there,
        step=wide_step,
    )
    own, x_top, x_bottom, y_top, y_bottom = rows_product(
        lefts,
        after(weight, far_top),
        column,
        (0, 2, 4),
        [(size, jnp.float32)]
        + [(half, t) for t in (jnp.bfloat16, jnp.float32, jnp.float32, jnp.bfloat16)],
        [(0, 0, size)] + [(i, 0, half) for i in range(1, 5)],
        rest_there,
    )
    return far_top, far_bottom, own, x_top, x_bottom, y_top, y_bottom


def scatter_send(parts):
    far_top, far_bottom, own, x_top, x_bottom, y_top, y_bottom = parts
    to_y = across(far_top, 1)
    to_x = across(far_bottom, 2)
    return own, across(x_top, 1), across(y_bottom, 2), to_x, to_y, x_bottom, y_top


def scatter_end(parts, beside=()):
    own, from_x_top, from_y_bottom, to_x, to_y, x_bottom, y_top = parts
    to_x, to_y = after((to_x, to_y), own, beside)
    x_bottom = low(x_bottom + wide(to_x))
    y_top = low(y_top + wide(to_y))
    return [own, from_x_top, across(x_bottom, 1), across(y_top, 2), from_y_bottom], (x_bottom, y_top)


def deal_out(values, spot, size, axis):
    got = []
    for j in range(CTX):
        piece = [
            lax.dynamic_slice_in_dim(v, (spot ^ j) * n, n, axis) for v, n in zip(values, size)
        ]
        piece = jnp.concatenate(piece, axis=axis) if len(piece) > 1 else piece[0]
        got.append(across(piece, j) if j else piece)
    return got


def gather_stages(shard):
    return lax.all_gather(shard, "fsdp", axis=0, tiled=True)


def sum_stages(values):
    return lax.psum_scatter(values, "fsdp", scatter_dimension=0, tiled=True)


def sum_small(values):
    count = lax.axis_size("fsdp")
    if count & (count - 1):
        return lax.psum(values, "fsdp")
    bit = 1
    while bit < count:
        values = values + lax.ppermute(values, "fsdp", [(i, i ^ bit) for i in range(count)])
        bit *= 2
    return values


def on_device(
    tokens,
    cotangent,
    lengths,
    deal,
    attn_gain,
    w_query,
    w_key,
    w_value,
    w_out,
    query_gain,
    key_gain,
    ffn_gain,
    w_gate,
    w_up,
    w_down,
):
    stages = lax.axis_size("fsdp")
    spot = lax.axis_index("ctx")
    core = lax.axis_index("tp")
    local_rows, width = tokens.shape
    head_size = query_gain.shape[0]
    half_rows = local_rows // 2
    heads = w_query.shape[1] // head_size // CTX
    query_cols = heads * head_size
    proj_cols = query_cols + 2 * head_size
    units = w_gate.shape[1] // CTX
    shard = width // stages // CTX

    def dealt_rows(values):
        got = [
            lax.dynamic_slice_in_dim(values, (spot ^ j) * shard, shard, 0) for j in range(CTX)
        ]
        return [across(v, j) if j else v for j, v in enumerate(got)]

    def whole_rows(both, half):
        return lax.dynamic_update_slice_in_dim(both, other_core(half), (1 - core) * half_rows, 0)

    def cut(pieces, start, size):
        return wide(in_order([p[:, start : start + size] for p in pieces], spot, 1))

    attn_scale = wide(attn_gain)[:, None]
    feed_scale = wide(ffn_gain)[:, None]
    scaled = [low(wide(w) * attn_scale) for w in (w_query, w_key, w_value)]
    dealt = deal_out(scaled + [w_out.T], spot, (query_cols, head_size, head_size, query_cols), 1)
    attn_weight = gather_stages(in_order(dealt, spot, 0))

    per_half = half_rows // BLK
    order = jnp.arange(deal.shape[1], dtype=jnp.int32).reshape(CTX, 2, per_half)
    chips = jnp.arange(CTX, dtype=jnp.int32) ^ spot
    cores = jnp.arange(2, dtype=jnp.int32) ^ core
    order = ((chips[:, None] * 2 + cores[None, :])[:, :, None] * per_half + order[0, 0]).reshape(-1)
    blocks = jnp.sum(
        jnp.where(order[:, None] == jnp.arange(order.shape[0])[None, :], deal[0][None, :], 0), axis=1
    )
    spots = jnp.arange(order.shape[0], dtype=jnp.int32)
    where_is = jnp.sum(
        jnp.where(blocks[None, :] == spots[:, None], spots[None, :], 0), axis=1
    ).astype(jnp.int32)
    info = jnp.concatenate([where_is, lengths])
    info, blocks = after((info, blocks), dealt)
    positions = (blocks[:, None] * BLK + jnp.arange(BLK, dtype=jnp.int32)[None, :]).reshape(-1)
    frequency = THETA ** (-(jnp.arange(head_size // 2, dtype=jnp.float32) * 2.0 / head_size))
    angles = wide(positions)[:, None] * frequency[None, :]
    cosine, sine = jnp.cos(angles), jnp.sin(angles)
    cosine = jnp.concatenate([cosine, cosine], axis=1)
    sine = jnp.concatenate([-sine, sine], axis=1)
    query_scale = wide(query_gain)[None, :]
    key_scale = wide(key_gain)[None, :]

    own = lax.dynamic_slice_in_dim(tokens, core * half_rows, half_rows, 0)
    inputs = wide(own)
    rstd = lax.rsqrt(jnp.mean(inputs * inputs, axis=1, keepdims=True) + EPS)
    normed_own = after(low(inputs * rstd), dealt)
    other, by_x, by_y = gather_near(normed_own)
    by_x, by_y = after((by_x, by_y), info, cosine, sine)
    feed_scaled = [low(wide(after(w, dealt)) * feed_scale) for w in (w_gate, w_up)]
    down_turned = after(w_down, dealt).T
    by_x, by_y = after((by_x, by_y), feed_scaled, down_turned)
    feed_dealt = deal_out(
        [after(w, by_x) for w in feed_scaled + [down_turned]], spot, (units,) * 3, 1
    )
    x_other, y_other, far_top, far_bottom = gather_far(by_x, by_y)
    far = [far_top, far_bottom, other_core(far_top), other_core(far_bottom)]
    normed = [normed_own, other, by_x, x_other, by_y, y_other] + far
    feed_weight = gather_stages(in_order([v[:, : 2 * units] for v in feed_dealt], spot, 0))
    down_weight = gather_stages(in_order([v[:, 2 * units :] for v in feed_dealt], spot, 0))

    valid = positions[:half_rows] < lengths[0]
    seed = lax.dynamic_slice_in_dim(cotangent, core * half_rows, half_rows, 0)
    seed = jnp.where(valid[:, None], seed, 0).astype(jnp.bfloat16)

    seed_other, seed_x, seed_y = gather_near(after(seed, far_top, far_bottom))
    proj, qkv, mixed_low, recip = attend_forward(
        info, normed, attn_weight, cosine, sine, query_scale, key_scale, heads
    )
    out_column = proj_cols // query_cols
    mixed_low, seed_x, seed_y = lax.optimization_barrier((mixed_low, seed_x, seed_y))
    seed_cross = [other_core(seed_x), other_core(seed_y)]
    parts = list(scatter_rows([mixed_low], attn_weight, out_column))
    parts[0], seed_cross = lax.optimization_barrier((parts[0], seed_cross))
    parts = scatter_send(parts)
    sums, _ = scatter_end(parts)
    hidden, hat_two = settle("norm", sums, (own,), (jnp.float32, jnp.bfloat16))

    total = local_rows * CTX
    other, by_x, by_y = gather_near(hat_two)
    x_other, y_other, far_top, far_bottom = gather_far(by_x, by_y)
    half = half_rows // 2
    seed_far = after((seed_x, seed_y), by_x, by_y)
    seed_far = [across(seed_far[0][:half], 2), across(seed_far[1][half:], 1)]
    filled = feed_expand([[hat_two, other]], 0, feed_weight, total)
    filled = feed_expand([[by_x, x_other], [by_y, y_other]], 1, feed_weight, total, filled)
    far = list(after((far_top, far_bottom), filled[0]))
    far += [other_core(v) for v in far]
    normed_two = [hat_two, other, by_x, x_other, by_y, y_other] + far
    seed_far = after(seed_far, filled[0])
    seeds = [seed, seed_other, seed_x, seed_cross[0], seed_y, seed_cross[1]]
    seeds += seed_far + [other_core(v) for v in seed_far]
    slope, silu, inner = feed_expand([far], 3, feed_weight, total, filled)
    grad_down = weight_terms([(seeds, [inner])])
    down_weight, grad_down = lax.optimization_barrier((down_weight, grad_down))
    grad_down = sum_stages(grad_down)
    dgate, dup = feed_back(seeds, down_weight, slope, silu)
    sums, sent = scatter_end(scatter_send(scatter_rows([dgate, dup], feed_weight, 0)))
    grad_feed = weight_terms([(normed_two, [after(dgate, sent), dup])])
    sums, grad_feed = lax.optimization_barrier((sums, grad_feed))
    grad_feed = sum_stages(after(grad_feed, grad_down))
    grad_hidden, grad_attn = settle("back", sums, (hidden, seed), (jnp.float32, jnp.bfloat16))

    other, by_x, by_y = gather_near(grad_attn)
    feed_parts = scatter_rows([after(inner, other)], down_weight, 0)
    by_x, by_y = after((by_x, by_y), feed_parts[:2], feed_parts[2])
    x_other, y_other, far_top, far_bottom = gather_far(by_x, by_y)
    far = [far_top, far_bottom, other_core(far_top), other_core(far_bottom)]
    grad_attn = [grad_attn, other, by_x, x_other, by_y, y_other] + far
    feed_parts = scatter_send(after(feed_parts, grad_attn[6:8]))
    grad_proj, gain_sums = attend_backward(
        info,
        grad_attn,
        attn_weight,
        proj,
        qkv,
        mixed_low,
        recip,
        cosine,
        sine,
        query_scale,
        key_scale,
        heads,
    )
    grad_proj, feed_parts = lax.optimization_barrier((grad_proj, feed_parts))
    down_pieces = dealt_rows(after(grad_down, grad_proj))
    grad_attn_w = weight_terms([(normed, [grad_proj]), (grad_attn, [mixed_low])])
    weight = after(attn_weight, grad_attn_w)
    grad_attn_w = sum_stages(after(grad_attn_w, grad_feed))
    feed_sums, feed_sent = scatter_end(feed_parts, down_pieces)
    feed_pieces = dealt_rows(after(grad_feed, feed_sent))
    parts = scatter_rows([grad_proj], after(weight, feed_sent), 0)
    sums, sent = scatter_end(scatter_send(parts), (feed_sums, feed_pieces))
    grad_gate_w = cut(feed_pieces, 0, units)
    grad_up_w = cut(feed_pieces, units, units)
    feed_gain = jnp.sum(wide(w_gate) * grad_gate_w + wide(w_up) * grad_up_w, axis=1)
    feed_gain = feed_gain + other_core(feed_gain)
    grad_gate_w = grad_gate_w * feed_scale
    grad_up_w = grad_up_w * feed_scale
    grad_down_w = cut(down_pieces, 0, units).T
    early = (grad_gate_w, grad_up_w, grad_down_w)
    sums, early, grad_attn_w = lax.optimization_barrier((sums, early, grad_attn_w))
    grad_gate_w, grad_up_w, grad_down_w = early
    proj_pieces = dealt_rows(grad_attn_w)
    tokens_half, grad_tokens = settle("back", sums, (own, grad_hidden), (jnp.float32,), core)
    feed_sums = after(feed_sums, tokens_half, proj_pieces)
    gain_sums = after(gain_sums, tokens_half)
    gain_sums = gain_sums + other_core(gain_sums)
    for bit in (1, 2):
        gain_sums = gain_sums + across(gain_sums, bit)
    gain_sums = sum_small(gain_sums)
    output_half, output = settle("add", feed_sums, (hidden,), (jnp.bfloat16,), core)

    output = whole_rows(output, output_half)
    grad_tokens = whole_rows(grad_tokens, tokens_half)
    grad_query_w = cut(proj_pieces, 0, query_cols)
    grad_key_w = cut(proj_pieces, query_cols, head_size)
    grad_value_w = cut(proj_pieces, query_cols + head_size, head_size)
    grad_out_w = cut(proj_pieces, proj_cols, query_cols).T

    pairs = ((w_query, grad_query_w), (w_key, grad_key_w), (w_value, grad_value_w))
    norm_gain = sum(jnp.sum(wide(w) * g, axis=1) for w, g in pairs)
    norm_gain = norm_gain + other_core(norm_gain)
    return (
        output,
        grad_tokens,
        norm_gain,
        grad_query_w * attn_scale,
        grad_key_w * attn_scale,
        grad_value_w * attn_scale,
        grad_out_w,
        gain_sums[0],
        gain_sums[1],
        feed_gain,
        grad_gate_w,
        grad_up_w,
        grad_down_w,
    )


def solution(mesh):
    return jax.shard_map(
        on_device,
        mesh=mesh,
        in_specs=(
            P(("fsdp", "ctx"), None),
            P(("fsdp", "ctx"), None),
            P("fsdp"),
            P("fsdp", None),
            P(("fsdp", "ctx")),
            P(("fsdp", "ctx"), "tp"),
            P(("fsdp", "ctx"), "tp"),
            P(("fsdp", "ctx"), "tp"),
            P("tp", ("fsdp", "ctx")),
            P(),
            P(),
            P(("fsdp", "ctx")),
            P(("fsdp", "ctx"), "tp"),
            P(("fsdp", "ctx"), "tp"),
            P("tp", ("fsdp", "ctx")),
        ),
        out_specs=(
            P(("fsdp", "ctx"), None),
            P(("fsdp", "ctx"), None),
            P(("fsdp", "ctx")),
            P(("fsdp", "ctx"), "tp"),
            P(("fsdp", "ctx"), "tp"),
            P(("fsdp", "ctx"), "tp"),
            P("tp", ("fsdp", "ctx")),
            P(),
            P(),
            P(("fsdp", "ctx")),
            P(("fsdp", "ctx"), "tp"),
            P(("fsdp", "ctx"), "tp"),
            P("tp", ("fsdp", "ctx")),
        ),
        check_vma=False,
    )
```
